256 devices in a mesh: gy: 16 (over y, x_hi, core), gz: 16 (over z, x_lo).
Axes of the slice: x: 4 (x_hi: 2, x_lo: 2; x = x_hi * 2 + x_lo), y: 4, z: 8, core: 2. Of those that a mesh axis runs over, the one named last changes fastest.
Arguments:
- labels: int32 [6, 4096, 2048], P(None, 'gy', 'gz'), may hold values from 0 to 5
- porosity: float32 [6], replicated, may hold values from 0 to 1
Outputs:
- spectra: float32 [4, 2, 4096, 2048], P(None, None, 'gy', 'gz')
The draws below stay inside these ranges and needn't reach their ends.
All inputs are finite; a program needn't handle non-finite values.
Results may differ from the reference program's by a relative error of at most 0.0003.
Values sent between devices are 32-bit elements; how exact they have to be, the bound alone decides.
No kernel may reach another device: no remote copies, remote signals or barrier semaphores. Data moves between devices by JAX's collectives and lax.ppermute only.
A program may use at most 128 MiB of HBM per device.

```python
import jax
import jax.numpy as jnp
from jax import lax

NY = 4096
NZ = 2048
NLAB = 6
XP = 6


def place_ends(array, key, smallest, high):
    shape = array.shape
    place = [jax.random.randint(jax.random.fold_in(key, axis), (), 0, shape[axis]) for axis in range(len(shape))]
    array = array.at[tuple(place)].set(smallest)
    longest = shape.index(max(shape))
    place[longest] = (place[longest] + 1) % shape[longest]
    return array.at[tuple(place)].set(high)


def setup_inputs(seed: int = 0) -> dict:
    seeds = jax.random.split(jax.random.key(seed), 3)
    labels = place_ends(jax.random.randint(seeds[0], (XP, NY, NZ), 0, NLAB), jax.random.fold_in(seeds[0], 1), 0, NLAB - 1).astype(jnp.int32)
    porosity = jnp.clip(jax.random.uniform(seeds[1], (NLAB,), jnp.float32, 0.0, 1.0), 0.0, 1.0)
    return {"labels": labels, "porosity": porosity}


def smooth_along(field, axis):
    extent = field.shape[axis]
    lower = lax.slice_in_dim(field, 0, extent - 2, axis=axis)
    middle = lax.slice_in_dim(field, 1, extent - 1, axis=axis)
    upper = lax.slice_in_dim(field, 2, extent, axis=axis)
    return (lower + 6.0 * middle + upper) * 0.125

def surface_pore(padded):
    smoothed = smooth_along(smooth_along(smooth_along(padded, 0), 1), 2)
    inner = smoothed[1:-1, 1:-1, 1:-1]
    grad_x = smoothed[2:, 1:-1, 1:-1] - smoothed[:-2, 1:-1, 1:-1]
    grad_y = smoothed[1:-1, 2:, 1:-1] - smoothed[1:-1, :-2, 1:-1]
    grad_z = smoothed[1:-1, 1:-1, 2:] - smoothed[1:-1, 1:-1, :-2]
    surface = jnp.sqrt(grad_x * grad_x + grad_y * grad_y + grad_z * grad_z + 0.01)
    return (surface, inner)

def reference(labels, porosity):
    filled = porosity[labels]
    padded = jnp.pad(filled, ((0, 0), (2, 2), (2, 2)), mode='wrap')
    surface, pore_field = surface_pore(padded)
    surf_hat = jnp.fft.fft2(surface, axes=(1, 2))
    pore_hat = jnp.fft.fft2(pore_field, axes=(1, 2))
    surf_re, surf_im = (jnp.real(surf_hat), jnp.imag(surf_hat))
    pore_re, pore_im = (jnp.real(pore_hat), jnp.imag(pore_hat))
    factor = 64.0 / (NY * NZ)
    spectra = jnp.stack([(surf_re * surf_re + surf_im * surf_im) * factor, (pore_re * pore_re + pore_im * pore_im) * factor, (surf_re * pore_re + surf_im * pore_im) * factor, (surf_im * pore_re - surf_re * pore_im) * factor]).astype(jnp.float32)
    spectra = spectra.at[:, :, 0, 0].set(0.0)
    return spectra
```

```python
import functools
import math

import jax
import jax.numpy as jnp
import ml_dtypes
import numpy as np
from jax import lax
from jax.experimental import pallas as pl
from jax.experimental.pallas import tpu as pltpu
from jax.sharding import PartitionSpec as P

VMEM = pl.BlockSpec(memory_space=pltpu.VMEM)
SMEM = pl.BlockSpec(memory_space=pltpu.SMEM)
PARAMS = pltpu.CompilerParams(vmem_limit_bytes=48 * 1024 * 1024)


def halves(matrix):
    high = matrix.astype(ml_dtypes.bfloat16)
    low = (matrix - high.astype(np.float64)).astype(ml_dtypes.bfloat16)
    return high, low


def split(value):
    high = value.astype(jnp.bfloat16)
    low = (value - high.astype(jnp.float32)).astype(jnp.bfloat16)
    return high, low


def dot(a, b):
    return lax.dot_general(a, b, (((1,), (0,)), ((), ())), preferred_element_type=jnp.float32)


def dot_t(a, b):
    return lax.dot_general(a, b, (((1,), (1,)), ((), ())), preferred_element_type=jnp.float32)


def z_matrices():
    q = np.arange(128)[:, None]
    j = np.arange(128)[None, :]

    def block(s, sign):
        theta = 2.0 * math.pi / 2048 * ((j * (16 * q + s)) % 2048)
        return np.concatenate([np.cos(theta), sign * np.sin(theta)], axis=1)

    entries = []
    for e in range(8):
        first = block(e, 1.0)
        second = block(8, 1.0) if e == 0 else block(16 - e, -1.0)
        high_a, low_a = halves(first)
        high_b, low_b = halves(second)
        entries.append(np.concatenate([high_a, high_b, low_a, low_b], axis=0))
    return np.stack(entries)


def y_matrix():
    m = np.arange(256)[:, None]
    i = np.arange(256)[None, :]
    theta = 2.0 * math.pi / 256 * ((m * i) % 256)
    high, low = halves(np.concatenate([np.cos(theta), np.sin(theta)], axis=0))
    return np.concatenate([high, low], axis=0)


def twiddles():
    m = np.arange(256)[:, None]
    r = np.arange(128)[None, :] % 16
    phi = 2.0 * math.pi / 4096 * (m * r)
    return np.cos(phi).astype(np.float32), (-np.sin(phi)).astype(np.float32)


def last_matrix():
    w = np.zeros((4, 2, 16, 2, 2, 2, 2, 16))
    g = np.arange(16)[:, None]
    r = np.arange(16)[None, :]
    psi = 2.0 * math.pi / 16 * ((g * r) % 16)
    cos, sin = np.cos(psi), np.sin(psi)
    for field in range(2):
        for plane in range(2):
            w[2 * field, plane, :, 0, 0, field, plane] = cos
            w[2 * field, plane, :, 1, 1, field, plane] = cos
            w[2 * field, plane, :, 0, 1, field, plane] = sin
            w[2 * field, plane, :, 1, 0, field, plane] = -sin
            w[2 * field + 1, plane, :, 0, 1, field, plane] = cos
            w[2 * field + 1, plane, :, 1, 0, field, plane] = -cos
            w[2 * field + 1, plane, :, 0, 0, field, plane] = -sin
            w[2 * field + 1, plane, :, 1, 1, field, plane] = -sin
    high, low = halves(w.reshape(128, 256))
    return np.concatenate([high, low], axis=0)


def rows_kernel(por_ref, lab_ref, up_ref, down_ref, out_ref, ext):
    def fill(ids):
        value = jnp.full(ids.shape, por_ref[0], jnp.float32)
        for k in range(1, 6):
            value = jnp.where(ids == k, por_ref[k], value)
        return value

    def along_x(ref):
        f = [fill(ref[x]) for x in range(6)]
        s = [(f[k] + 6.0 * f[k + 1] + f[k + 2]) * 0.125 for k in range(4)]
        return [s[2] - s[0], s[3] - s[1], s[1], s[2]]

    for a, value in enumerate(along_x(lab_ref)):
        ext[a, 8:264, :] = value
    for a, value in enumerate(along_x(up_ref)):
        ext[a, 6:8, :] = value
    for a, value in enumerate(along_x(down_ref)):
        ext[a, 264:266, :] = value
    for a in range(4):
        main = (ext[a, 7:263, :] + 6.0 * ext[a, 8:264, :] + ext[a, 9:265, :]) * 0.125
        out_ref[:, 16 * a : 16 * a + 16, :] = main.reshape(16, 16, 128)
    for p in range(2):
        a = 2 + p
        first = (ext[a, 6:7, :] + 6.0 * ext[a, 7:8, :] + ext[a, 8:9, :]) * 0.125
        last = (ext[a, 263:264, :] + 6.0 * ext[a, 264:265, :] + ext[a, 265:266, :]) * 0.125
        for d in range(16):
            below = first if d == 0 else out_ref[d - 1, 16 * a + 15 : 16 * a + 16, :]
            above = last if d == 15 else out_ref[d + 1, 16 * a : 16 * a + 1, :]
            out_ref[d, 64 + 2 * p : 65 + 2 * p, :] = below
            out_ref[d, 65 + 2 * p : 66 + 2 * p, :] = above
    out_ref[:, 68:72, :] = jnp.zeros((16, 4, 128), jnp.float32)


def real_transform(x):
    n = len(x)
    if n == 2:
        return [(x[0] + x[1], None), (x[0] - x[1], None)]
    even = real_transform(x[0::2])
    odd = real_transform(x[1::2])
    out = [None] * (n // 2 + 1)
    for k in range(n // 4 + 1):
        (er, ei), (dr, di) = even[k], odd[k]
        c, s = math.cos(2.0 * math.pi * k / n), math.sin(2.0 * math.pi * k / n)
        if k == 0:
            out[0] = (er + dr, None)
            out[n // 2] = (er - dr, None)
        elif 4 * k == n:
            out[k] = (er, -dr)
        else:
            tr = c * dr if di is None else c * dr + s * di
            ti = -s * dr if di is None else c * di - s * dr
            out[k] = (er + tr, ti if ei is None else ei + ti)
            out[n // 2 - k] = (er - tr, ti if ei is None else ti - ei)
    return out


def columns_kernel(in_ref, w_ref, out_ref, ext, x_ref):
    lane = lax.broadcasted_iota(jnp.int32, (16, 16, 128), 2)

    def before(x):
        rolled = pltpu.roll(x, 1, 2)
        return jnp.where(lane == 0, jnp.concatenate([rolled[15:], rolled[:15]], axis=0), rolled)

    def after(x):
        rolled = pltpu.roll(x, 127, 2)
        return jnp.where(lane == 127, jnp.concatenate([rolled[1:], rolled[:1]], axis=0), rolled)

    def along_z(x):
        return (before(x) + 6.0 * x + after(x)) * 0.125

    for p in range(2):
        center = in_ref[:, 32 + 16 * p : 48 + 16 * p, :]
        ext[:, 8:24, :] = center
        ext[:, 7:8, :] = in_ref[:, 64 + 2 * p : 65 + 2 * p, :]
        ext[:, 24:25, :] = in_ref[:, 65 + 2 * p : 66 + 2 * p, :]
        grad_x = along_z(in_ref[:, 16 * p : 16 * p + 16, :])
        grad_y = along_z(ext[:, 9:25, :] - ext[:, 7:23, :])
        pore = along_z(center)
        grad_z = after(pore) - before(pore)
        surface = jnp.sqrt(grad_x * grad_x + grad_y * grad_y + grad_z * grad_z + 0.01)
        x_ref[:, 16 * p : 16 * p + 16, :] = surface
        x_ref[:, 32 + 16 * p : 48 + 16 * p, :] = pore
    parts = real_transform([x_ref[d] for d in range(16)])
    sign = jnp.where(lax.broadcasted_iota(jnp.int32, (128, 128), 1) < 64, 1.0, -1.0)

    def arranged(k):
        re, im = parts[k]
        if im is None:
            im = jnp.zeros_like(re)
        top = jnp.concatenate([re, im], axis=1)
        bottom = jnp.concatenate([im, -re], axis=1)
        return split(jnp.concatenate([top, bottom], axis=0))

    for k in (0, 8):
        high, low = arranged(k)
        at = 16 * k
        lead = w_ref[0, at : at + 128, :]
        tail = w_ref[0, at + 256 : at + 384, :]
        out_ref[k] = dot_t(lead, high) + dot_t(tail, high) + dot_t(lead, low)
    for k in range(1, 8):
        high, low = arranged(k)
        main = dot_t(w_ref[k], high)
        both = main[:256] + main[256:] + dot_t(w_ref[k, :256, :], low)
        out_ref[k] = both[:128]
        out_ref[16 - k] = both[128:] * sign


def spectra_kernel(in_ref, y_ref, tr_ref, ti_ref, last_ref, out_ref):
    factor = 64.0 / (4096 * 2048)
    for q in range(8):
        high, low = split(in_ref[pl.ds(q, 256, stride=8), :])
        main = dot(y_ref[...], high)
        both = main[:512] + main[512:] + dot(y_ref[:512, :], low)
        cos, sin = both[:256], both[256:]
        tr, ti = tr_ref[...], ti_ref[...]
        mixed = jnp.concatenate([cos * tr + sin * ti, sin * tr - cos * ti], axis=1)
        high, low = split(mixed)
        main = dot_t(last_ref[...], high)
        modes = main[:128] + main[128:] + dot_t(last_ref[:128, :], low)
        sr, si, pr, pi = modes[:32], modes[32:64], modes[64:96], modes[96:]
        results = (
            (sr * sr + si * si) * factor,
            (pr * pr + pi * pi) * factor,
            (sr * pr + si * pi) * factor,
            (si * pr - sr * pi) * factor,
        )
        for o, result in enumerate(results):
            for p in range(2):
                for half in range(2):
                    start = 8 * (2 * q + half) + 2 * o + p
                    block = result[16 * p : 16 * p + 16, 128 * half : 128 * half + 128]
                    out_ref[pl.ds(start, 16, stride=128), :] = block


def order_kernel(first_ref, in_ref, out_ref):
    row = lax.broadcasted_iota(jnp.int32, (128, 128), 0)
    col = lax.broadcasted_iota(jnp.int32, (128, 128), 1)
    drop = jnp.logical_and(row + col == 0, first_ref[0] == 1)
    for o in range(8):
        for half in range(2):
            parts = [in_ref[pl.ds(8 * (2 * q + half) + o, 16, stride=128), :] for q in range(8)]
            block = jnp.concatenate(parts, axis=0).T
            if half == 0:
                block = jnp.where(drop, 0.0, block)
            out_ref[o, 128 * half : 128 * half + 128, :] = block


def shape(*sizes):
    return jax.ShapeDtypeStruct(sizes, jnp.float32)


def shards(labels, porosity):
    count = lax.axis_size("gy")
    up = lax.ppermute(labels[:, -2:, :], "gy", [(i, (i + 1) % count) for i in range(count)])
    down = lax.ppermute(labels[:, :2, :], "gy", [((i + 1) % count, i) for i in range(count)])
    rows = pl.pallas_call(
        rows_kernel,
        out_shape=shape(16, 72, 128),
        in_specs=[SMEM, VMEM, VMEM, VMEM],
        out_specs=VMEM,
        scratch_shapes=[pltpu.VMEM((4, 272, 128), jnp.float32)],
        compiler_params=PARAMS,
        name="rows",
    )(porosity, labels, up, down)
    rows = lax.all_to_all(rows, "gz", 0, 0, tiled=True)
    columns = pl.pallas_call(
        columns_kernel,
        out_shape=shape(16, 128, 128),
        in_specs=[VMEM, VMEM],
        out_specs=VMEM,
        scratch_shapes=[pltpu.VMEM((16, 32, 128), jnp.float32), pltpu.VMEM((16, 64, 128), jnp.float32)],
        compiler_params=PARAMS,
        name="columns",
    )(rows, jnp.asarray(z_matrices()))
    columns = lax.all_to_all(columns.reshape(256, 8, 128), ("gy", "gz"), 0, 0, tiled=True)
    cos, sin = twiddles()
    spectra = pl.pallas_call(
        spectra_kernel,
        out_shape=shape(2048, 128),
        in_specs=[VMEM] * 5,
        out_specs=VMEM,
        compiler_params=PARAMS,
        name="spectra",
    )(columns.reshape(2048, 128), jnp.asarray(y_matrix()), jnp.asarray(cos), jnp.asarray(sin), jnp.asarray(last_matrix()))
    spectra = lax.all_to_all(spectra.reshape(16, 128, 128), "gy", 0, 0, tiled=True)
    origin = jnp.logical_and(lax.axis_index("gy") == 0, lax.axis_index("gz") == 0).astype(jnp.int32).reshape(1)
    result = pl.pallas_call(
        order_kernel,
        out_shape=shape(8, 256, 128),
        in_specs=[SMEM, VMEM],
        out_specs=VMEM,
        compiler_params=PARAMS,
        name="order",
    )(origin, spectra.reshape(2048, 128))
    return result.reshape(4, 2, 256, 128)


def solution(mesh):
    placed = (P(None, "gy", "gz"), P())
    return jax.shard_map(
        shards, mesh=mesh, in_specs=placed, out_specs=P(None, None, "gy", "gz"), check_vma=False
    )
```

```python
import functools
import math

import jax
import jax.numpy as jnp
import ml_dtypes
import numpy as np
from jax import lax
from jax.experimental import pallas as pl
from jax.experimental.pallas import tpu as pltpu
from jax.sharding import PartitionSpec as P

VMEM = pl.BlockSpec(memory_space=pltpu.VMEM)
SMEM = pl.BlockSpec(memory_space=pltpu.SMEM)
PARAMS = pltpu.CompilerParams(vmem_limit_bytes=48 * 1024 * 1024)


def halves(matrix):
    high = matrix.astype(ml_dtypes.bfloat16)
    low = (matrix - high.astype(np.float64)).astype(ml_dtypes.bfloat16)
    return high, low


def split(value):
    high = value.astype(jnp.bfloat16)
    low = (value - high.astype(jnp.float32)).astype(jnp.bfloat16)
    return high, low


def dot(a, b):
    return lax.dot_general(a, b, (((1,), (0,)), ((), ())), preferred_element_type=jnp.float32)


def dot_t(a, b):
    return lax.dot_general(a, b, (((1,), (1,)), ((), ())), preferred_element_type=jnp.float32)


def z_matrices():
    q = np.arange(128)[:, None]
    j = np.arange(128)[None, :]

    def block(s, sign):
        theta = 2.0 * math.pi / 2048 * ((j * (16 * q + s)) % 2048)
        return np.concatenate([np.cos(theta), sign * np.sin(theta)], axis=1)

    entries = []
    for e in range(8):
        first = block(e, 1.0)
        second = block(8, 1.0) if e == 0 else block(16 - e, -1.0)
        high_a, low_a = halves(first)
        high_b, low_b = halves(second)
        entries.append(np.concatenate([high_a, high_b, low_a, low_b], axis=0))
    return np.stack(entries)


def joined(matrix, axis):
    high, low = halves(matrix)
    return np.concatenate([high, low, high], axis=axis)


def y_matrix():
    i = np.arange(256)[:, None]
    m = np.arange(256)[None, :]
    theta = 2.0 * math.pi / 256 * ((i * m) % 256)
    return joined(np.concatenate([np.cos(theta), np.sin(theta)], axis=1), 0)


def twiddles():
    r = np.arange(128)[:, None] % 16
    m = np.arange(256)[None, :]
    phi = 2.0 * math.pi / 4096 * (m * r)
    return np.cos(phi).astype(np.float32), (-np.sin(phi)).astype(np.float32)


def last_matrix():
    w = np.zeros((4, 2, 16, 2, 2, 2, 2, 16))
    g = np.arange(16)[:, None]
    r = np.arange(16)[None, :]
    psi = 2.0 * math.pi / 16 * ((g * r) % 16)
    cos, sin = np.cos(psi), np.sin(psi)
    for field in range(2):
        for plane in range(2):
            w[2 * field, plane, :, 0, 0, field, plane] = cos
            w[2 * field, plane, :, 1, 1, field, plane] = cos
            w[2 * field, plane, :, 0, 1, field, plane] = sin
            w[2 * field, plane, :, 1, 0, field, plane] = -sin
            w[2 * field + 1, plane, :, 0, 1, field, plane] = cos
            w[2 * field + 1, plane, :, 1, 0, field, plane] = -cos
            w[2 * field + 1, plane, :, 0, 0, field, plane] = -sin
            w[2 * field + 1, plane, :, 1, 1, field, plane] = -sin
    return joined(w.reshape(128, 256), 1)


def along_x(por_ref, labels):
    def fill(ids):
        value = jnp.full(ids.shape, por_ref[0], jnp.float32)
        for k in range(1, 6):
            value = jnp.where(ids == k, por_ref[k], value)
        return value

    f = [fill(ids) for ids in labels]
    s = [(f[k] + 6.0 * f[k + 1] + f[k + 2]) * 0.125 for k in range(4)]
    return [s[2] - s[0], s[3] - s[1], s[1], s[2]]


BLOCKS = 4
TALL = 256 // BLOCKS


def planes_kernel(por_ref, lab_ref, out_ref, held, sems):
    copies = []
    for b in range(BLOCKS):
        rows = pl.ds(TALL * b, TALL)
        copies.append(pltpu.make_async_copy(lab_ref.at[:, rows, :], held.at[:, rows, :], sems.at[b]))
        copies[-1].start()
    for b in range(BLOCKS):
        copies[b].wait()
        rows = pl.ds(TALL * b, TALL)
        for a, value in enumerate(along_x(por_ref, [held[x, rows, :] for x in range(6)])):
            out_ref[a, rows, :] = value


def rows_kernel(por_ref, in_ref, next_ref, out_ref, ext):
    ext[:, 0:256, :] = in_ref[...]
    for a, value in enumerate(along_x(por_ref, [next_ref[x] for x in range(6)])):
        ext[a, 256:260, :] = value

    def along_y(a, first, count):
        return (
            ext[a, first - 1 : first - 1 + count, :]
            + 6.0 * ext[a, first : first + count, :]
            + ext[a, first + 1 : first + 1 + count, :]
        ) * 0.125

    for a in range(4):
        out_ref[:, 16 * a : 16 * a + 16, :] = along_y(a, 2, 256).reshape(16, 16, 128)
    for p in range(2):
        a = 2 + p
        for d in range(16):
            below = along_y(a, 1, 1) if d == 0 else out_ref[d - 1, 16 * a + 15 : 16 * a + 16, :]
            above = along_y(a, 258, 1) if d == 15 else out_ref[d + 1, 16 * a : 16 * a + 1, :]
            out_ref[d, 64 + 2 * p : 65 + 2 * p, :] = below
            out_ref[d, 65 + 2 * p : 66 + 2 * p, :] = above
    out_ref[:, 68:72, :] = jnp.zeros((16, 4, 128), jnp.float32)


def real_transform(x):
    n = len(x)
    if n == 2:
        return [(x[0] + x[1], None), (x[0] - x[1], None)]
    even = real_transform(x[0::2])
    odd = real_transform(x[1::2])
    out = [None] * (n // 2 + 1)
    for k in range(n // 4 + 1):
        (er, ei), (dr, di) = even[k], odd[k]
        c, s = math.cos(2.0 * math.pi * k / n), math.sin(2.0 * math.pi * k / n)
        if k == 0:
            out[0] = (er + dr, None)
            out[n // 2] = (er - dr, None)
        elif 4 * k == n:
            out[k] = (er, -dr)
        else:
            tr = c * dr if di is None else c * dr + s * di
            ti = -s * dr if di is None else c * di - s * dr
            out[k] = (er + tr, ti if ei is None else ei + ti)
            out[n // 2 - k] = (er - tr, ti if ei is None else ti - ei)
    return out


def columns_kernel(in_ref, w_ref, out_ref, ext, x_ref):
    lane = lax.broadcasted_iota(jnp.int32, (16, 16, 128), 2)

    def before(x):
        rolled = pltpu.roll(x, 1, 2)
        return jnp.where(lane == 0, jnp.concatenate([rolled[15:], rolled[:15]], axis=0), rolled)

    def after(x):
        rolled = pltpu.roll(x, 127, 2)
        return jnp.where(lane == 127, jnp.concatenate([rolled[1:], rolled[:1]], axis=0), rolled)

    def along_z(x):
        return (before(x) + 6.0 * x + after(x)) * 0.125

    for p in range(2):
        center = in_ref[:, 32 + 16 * p : 48 + 16 * p, :]
        ext[:, 8:24, :] = center
        ext[:, 7:8, :] = in_ref[:, 64 + 2 * p : 65 + 2 * p, :]
        ext[:, 24:25, :] = in_ref[:, 65 + 2 * p : 66 + 2 * p, :]
        grad_x = along_z(in_ref[:, 16 * p : 16 * p + 16, :])
        grad_y = along_z(ext[:, 9:25, :] - ext[:, 7:23, :])
        pore = along_z(center)
        grad_z = after(pore) - before(pore)
        surface = jnp.sqrt(grad_x * grad_x + grad_y * grad_y + grad_z * grad_z + 0.01)
        x_ref[:, 16 * p : 16 * p + 16, :] = surface
        x_ref[:, 32 + 16 * p : 48 + 16 * p, :] = pore
    parts = real_transform([x_ref[d] for d in range(16)])
    sign = jnp.where(lax.broadcasted_iota(jnp.int32, (128, 128), 1) < 64, 1.0, -1.0)

    def arranged(k):
        re, im = parts[k]
        if im is None:
            im = jnp.zeros_like(re)
        top = jnp.concatenate([re, im], axis=1)
        bottom = jnp.concatenate([im, -re], axis=1)
        return split(jnp.concatenate([top, bottom], axis=0))

    for k in (0, 8):
        high, low = arranged(k)
        at = 16 * k
        lead = w_ref[0, at : at + 128, :]
        tail = w_ref[0, at + 256 : at + 384, :]
        out_ref[k] = dot_t(lead, high) + dot_t(tail, high) + dot_t(lead, low)
    for k in range(1, 8):
        high, low = arranged(k)
        main = dot_t(w_ref[k], high)
        both = main[:256] + main[256:] + dot_t(w_ref[k, :256, :], low)
        out_ref[k] = both[:128]
        out_ref[16 - k] = both[128:] * sign


def modes_kernel(in_ref, y_ref, tr_ref, ti_ref, last_ref, out_ref):
    tr, ti = tr_ref[...], ti_ref[...]
    for pair in range(4):
        turned = jnp.concatenate([in_ref[pl.ds(2 * pair + h, 256, stride=8), :].T for h in range(2)], axis=0)
        high, low = split(turned)
        both = dot(jnp.concatenate([high, high, low], axis=1), y_ref[...])
        for h in range(2):
            q = 2 * pair + h
            cos, sin = both[128 * h : 128 * h + 128, :256], both[128 * h : 128 * h + 128, 256:]
            high, low = split(jnp.concatenate([cos * tr + sin * ti, sin * tr - cos * ti], axis=0))
            modes = dot(last_ref[...], jnp.concatenate([high, high, low], axis=0))
            sr, si, pr, pi = modes[:32], modes[32:64], modes[64:96], modes[96:]
            square = sr * sr + si * si
            some = square > 1e-30
            scale = lax.rsqrt(jnp.maximum(square, 1e-30))
            results = (
                square * scale,
                jnp.where(some, (sr * pr + si * pi) * scale, jnp.sqrt(pr * pr + pi * pi)),
                jnp.where(some, (si * pr - sr * pi) * scale, 0.0),
            )
            for o, result in enumerate(results):
                for p in range(2):
                    for half in range(2):
                        block = result[16 * p : 16 * p + 16, 128 * half : 128 * half + 128]
                        out_ref[pl.ds(place(o, p, half, q), 16, stride=96), :] = block


def place(o, p, half, q):
    return 32 * o + 16 * p + 8 * half + q


def spectra_kernel(in_ref, out_ref):
    factor = 64.0 / (4096 * 2048)
    row = lax.broadcasted_iota(jnp.int32, (128, 128), 0)
    col = lax.broadcasted_iota(jnp.int32, (128, 128), 1)
    device = lax.axis_index("gy") + lax.axis_index("gz")
    drop = row + col + device == 0
    for p in range(2):
        for half in range(2):
            size, re, im = [
                jnp.concatenate([in_ref[pl.ds(place(o, p, half, q), 16, stride=96), :] for q in range(8)], axis=0).T
                for o in range(3)
            ]
            scaled = size * factor
            results = (size * scaled, (re * re + im * im) * factor, scaled * re, scaled * im)
            for o, result in enumerate(results):
                if half == 0:
                    result = jnp.where(drop, 0.0, result)
                out_ref[o, p, 128 * half : 128 * half + 128, :] = result


def shape(*sizes):
    return jax.ShapeDtypeStruct(sizes, jnp.float32)


def shards(labels, porosity):
    count = lax.axis_size("gy")
    following = lax.ppermute(labels[:, :4, :], "gy", [((i + 1) % count, i) for i in range(count)])
    planes = pl.pallas_call(
        planes_kernel,
        out_shape=shape(4, 256, 128),
        in_specs=[SMEM, pl.BlockSpec(memory_space=pl.ANY)],
        out_specs=VMEM,
        scratch_shapes=[pltpu.VMEM((6, 256, 128), jnp.int32), pltpu.SemaphoreType.DMA((BLOCKS,))],
        compiler_params=PARAMS,
        cost_estimate=pl.CostEstimate(flops=10_000_000, bytes_accessed=4_000_000, transcendentals=0),
        name="planes",
    )(porosity, labels)
    rows = pl.pallas_call(
        rows_kernel,
        out_shape=shape(16, 72, 128),
        in_specs=[SMEM, VMEM, VMEM],
        out_specs=VMEM,
        scratch_shapes=[pltpu.VMEM((4, 264, 128), jnp.float32)],
        compiler_params=PARAMS,
        name="rows",
    )(porosity, planes, following)
    rows = lax.all_to_all(rows, "gz", 0, 0, tiled=True)
    columns = pl.pallas_call(
        columns_kernel,
        out_shape=shape(16, 128, 128),
        in_specs=[VMEM, VMEM],
        out_specs=VMEM,
        scratch_shapes=[pltpu.VMEM((16, 32, 128), jnp.float32), pltpu.VMEM((16, 64, 128), jnp.float32)],
        compiler_params=PARAMS,
        name="columns",
    )(rows, jnp.asarray(z_matrices()))
    columns = lax.all_to_all(columns.reshape(256, 8, 128), ("gy", "gz"), 0, 0, tiled=True)
    cos, sin = twiddles()
    modes = pl.pallas_call(
        modes_kernel,
        out_shape=shape(16 * 96, 128),
        in_specs=[VMEM] * 5,
        out_specs=VMEM,
        compiler_params=PARAMS,
        name="modes",
    )(columns.reshape(2048, 128), jnp.asarray(y_matrix()), jnp.asarray(cos), jnp.asarray(sin), jnp.asarray(last_matrix()))
    modes = lax.all_to_all(modes.reshape(16, 96, 128), "gy", 0, 0, tiled=True)
    return pl.pallas_call(
        spectra_kernel,
        out_shape=shape(4, 2, 256, 128),
        in_specs=[VMEM],
        out_specs=VMEM,
        compiler_params=PARAMS,
        name="spectra",
    )(modes.reshape(16 * 96, 128))


def solution(mesh):
    placed = (P(None, "gy", "gz"), P())
    return jax.shard_map(
        shards, mesh=mesh, in_specs=placed, out_specs=P(None, None, "gy", "gz"), check_vma=False
    )
```

```python
import functools
import math

import jax
import jax.numpy as jnp
import ml_dtypes
import numpy as np
from jax import lax
from jax.experimental import pallas as pl
from jax.experimental.pallas import tpu as pltpu
from jax.sharding import PartitionSpec as P

VMEM = pl.BlockSpec(memory_space=pltpu.VMEM)
HBM = pl.BlockSpec(memory_space=pltpu.HBM)
WIDE = pltpu.CompilerParams(vmem_limit_bytes=54000 * 1024)
PARAMS = pltpu.CompilerParams(vmem_limit_bytes=48 * 1024 * 1024)


def halves(matrix):
    high = matrix.astype(ml_dtypes.bfloat16)
    low = (matrix - high.astype(np.float64)).astype(ml_dtypes.bfloat16)
    return high, low


def split(value):
    high = value.astype(jnp.bfloat16)
    low = (value - high.astype(jnp.float32)).astype(jnp.bfloat16)
    return high, low


def dot(a, b):
    return lax.dot_general(a, b, (((1,), (0,)), ((), ())), preferred_element_type=jnp.float32)


def dot_t(a, b):
    return lax.dot_general(a, b, (((1,), (1,)), ((), ())), preferred_element_type=jnp.float32)


def joined(matrix, axis):
    high, low = halves(matrix)
    return np.concatenate([high, low, high], axis=axis)


def z_matrices():
    q = np.arange(128)[:, None]
    j = np.arange(128)[None, :]

    def block(s, sign):
        theta = 2.0 * math.pi / 2048 * ((j * (16 * q + s)) % 2048)
        return np.concatenate([np.cos(theta), sign * np.sin(theta)], axis=1)

    pairs = [(block(0, 1.0), block(8, 1.0))] + [(block(s, 1.0), block(16 - s, -1.0)) for s in range(1, 8)]
    return np.stack([joined(np.concatenate(pair, axis=0), 1) for pair in pairs])


def y_matrix():
    i = np.arange(256)[:, None]
    m = np.arange(256)[None, :]
    theta = 2.0 * math.pi / 256 * ((i * m) % 256)
    return joined(np.concatenate([np.cos(theta), np.sin(theta)], axis=1), 0)


def twiddles():
    r = np.arange(128)[:, None] % 16
    m = np.arange(256)[None, :]
    phi = 2.0 * math.pi / 4096 * (m * r)
    return np.cos(phi).astype(np.float32), (-np.sin(phi)).astype(np.float32)


def last_matrix():
    w = np.zeros((4, 2, 16, 2, 2, 2, 2, 16))
    g = np.arange(16)[:, None]
    r = np.arange(16)[None, :]
    psi = 2.0 * math.pi / 16 * ((g * r) % 16)
    cos, sin = np.cos(psi), np.sin(psi)
    for field in range(2):
        for plane in range(2):
            w[2 * field, plane, :, 0, 0, field, plane] = cos
            w[2 * field, plane, :, 1, 1, field, plane] = cos
            w[2 * field, plane, :, 0, 1, field, plane] = sin
            w[2 * field, plane, :, 1, 0, field, plane] = -sin
            w[2 * field + 1, plane, :, 0, 1, field, plane] = cos
            w[2 * field + 1, plane, :, 1, 0, field, plane] = -cos
            w[2 * field + 1, plane, :, 0, 0, field, plane] = -sin
            w[2 * field + 1, plane, :, 1, 1, field, plane] = -sin
    return joined(w.reshape(128, 256), 1)


def along_x(values, labels):
    def fill(ids):
        value = jnp.where(ids == 1, values[1], values[0])
        for k in range(2, 6):
            value = jnp.where(ids == k, values[k], value)
        return value

    f = [fill(ids) for ids in labels]
    s = [(f[k] + 6.0 * f[k + 1] + f[k + 2]) * 0.125 for k in range(4)]
    return [s[2] - s[0], s[3] - s[1], s[1], s[2]]


def along_y(ext, a, first, count):
    return (
        ext[a, first + 1 : first + 1 + count, :]
        + 6.0 * ext[a, first + 2 : first + 2 + count, :]
        + ext[a, first + 3 : first + 3 + count, :]
    ) * 0.125


BLOCKS = 4
TALL = 256 // BLOCKS


def planes_kernel(por_ref, lab_ref, out_ref, end_ref, table_ref, held, few, ext, sems):
    copies = [pltpu.make_async_copy(por_ref, few, sems.at[BLOCKS])]
    for b in range(BLOCKS):
        rows = pl.ds(TALL * b, TALL)
        copies.append(pltpu.make_async_copy(lab_ref.at[:, rows, :], held.at[:, rows, :], sems.at[b]))
    for copy in copies:
        copy.start()
    copies[0].wait()
    values = [few[k] for k in range(6)]
    for k in range(6):
        table_ref[k : k + 1, :] = jnp.full((1, 128), values[k], jnp.float32)
    table_ref[6:8, :] = jnp.zeros((2, 128), jnp.float32)
    done = 0
    for b in range(BLOCKS):
        copies[1 + b].wait()
        rows = pl.ds(TALL * b, TALL)
        for a, value in enumerate(along_x(values, [held[x, rows, :] for x in range(6)])):
            ext[a, rows, :] = value
        ready = (TALL * (b + 1) - 3) // 16
        for a in range(4):
            block = along_y(ext, a, 16 * done, 16 * (ready - done))
            out_ref[done:ready, 16 * a : 16 * a + 16, :] = block.reshape(ready - done, 16, 128)
        done = ready
    for p in range(2):
        a = 2 + p
        for d in range(15):
            below = along_y(ext, a, -1, 1) if d == 0 else out_ref[d - 1, 16 * a + 15 : 16 * a + 16, :]
            above = along_y(ext, a, 240, 1) if d == 14 else out_ref[d + 1, 16 * a : 16 * a + 1, :]
            out_ref[d, 64 + 2 * p : 65 + 2 * p, :] = below
            out_ref[d, 65 + 2 * p : 66 + 2 * p, :] = above
    out_ref[0:15, 68:72, :] = jnp.zeros((15, 4, 128), jnp.float32)
    out_ref[15] = jnp.zeros((72, 128), jnp.float32)
    end_ref[...] = ext[:, 232:256, :]


def rows_kernel(in_ref, end_ref, table_ref, next_ref, out_ref, ext):
    out_ref[0:15] = in_ref[0:15]
    ext[:, 0:24, :] = end_ref[...]
    values = [table_ref[k : k + 1, :] for k in range(6)]
    for a, value in enumerate(along_x(values, [next_ref[x] for x in range(6)])):
        ext[a, 24:28, :] = value
        out_ref[15, 16 * a : 16 * a + 16, :] = along_y(ext, a, 8, 16)
    for p in range(2):
        a = 2 + p
        out_ref[15, 64 + 2 * p : 65 + 2 * p, :] = along_y(ext, a, 7, 1)
        out_ref[15, 65 + 2 * p : 66 + 2 * p, :] = along_y(ext, a, 24, 1)
    out_ref[15, 68:72, :] = jnp.zeros((4, 128), jnp.float32)


def real_transform(x):
    n = len(x)
    if n == 2:
        return [(x[0] + x[1], None), (x[0] - x[1], None)]
    even = real_transform(x[0::2])
    odd = real_transform(x[1::2])
    out = [None] * (n // 2 + 1)
    for k in range(n // 4 + 1):
        (er, ei), (dr, di) = even[k], odd[k]
        c, s = math.cos(2.0 * math.pi * k / n), math.sin(2.0 * math.pi * k / n)
        if k == 0:
            out[0] = (er + dr, None)
            out[n // 2] = (er - dr, None)
        elif 4 * k == n:
            out[k] = (er, -dr)
        else:
            tr = c * dr if di is None else c * dr + s * di
            ti = -s * dr if di is None else c * di - s * dr
            out[k] = (er + tr, ti if ei is None else ei + ti)
            out[n // 2 - k] = (er - tr, ti if ei is None else ti - ei)
    return out


def columns_kernel(in_ref, w_ref, out_ref, ext, x_ref):
    lane = lax.broadcasted_iota(jnp.int32, (16, 16, 128), 2)

    def before(x):
        rolled = pltpu.roll(x, 1, 2)
        return jnp.where(lane == 0, jnp.concatenate([rolled[15:], rolled[:15]], axis=0), rolled)

    def after(x):
        rolled = pltpu.roll(x, 127, 2)
        return jnp.where(lane == 127, jnp.concatenate([rolled[1:], rolled[:1]], axis=0), rolled)

    def along_z(x):
        return (before(x) + 6.0 * x + after(x)) * 0.125

    for p in range(2):
        center = in_ref[:, 32 + 16 * p : 48 + 16 * p, :]
        ext[:, 8:24, :] = center
        ext[:, 7:8, :] = in_ref[:, 64 + 2 * p : 65 + 2 * p, :]
        ext[:, 24:25, :] = in_ref[:, 65 + 2 * p : 66 + 2 * p, :]
        grad_x = along_z(in_ref[:, 16 * p : 16 * p + 16, :])
        grad_y = along_z(ext[:, 9:25, :] - ext[:, 7:23, :])
        pore = along_z(center)
        grad_z = after(pore) - before(pore)
        surface = jnp.sqrt(grad_x * grad_x + grad_y * grad_y + grad_z * grad_z + 0.01)
        x_ref[:, 16 * p : 16 * p + 16, :] = surface
        x_ref[:, 32 + 16 * p : 48 + 16 * p, :] = pore
    parts = real_transform([x_ref[d] for d in range(16)])
    sign = jnp.where(lax.broadcasted_iota(jnp.int32, (128, 128), 1) < 64, 1.0, -1.0)

    def arranged(k):
        re, im = parts[k]
        if im is None:
            im = jnp.zeros_like(re)
        top = jnp.concatenate([re, im], axis=1)
        bottom = jnp.concatenate([im, -re], axis=1)
        high, low = split(jnp.concatenate([top, bottom], axis=0))
        return jnp.concatenate([high, high, low], axis=1)

    out_ref[0] = dot_t(w_ref[0, :128, :], arranged(0))
    out_ref[8] = dot_t(w_ref[0, 128:, :], arranged(8))
    for k in range(1, 8):
        both = dot_t(w_ref[k], arranged(k))
        out_ref[k] = both[:128]
        out_ref[16 - k] = both[128:] * sign


def modes_kernel(in_ref, y_ref, tr_ref, ti_ref, last_ref, out_ref):
    tr, ti = tr_ref[...], ti_ref[...]
    turned = jnp.concatenate([in_ref[pl.ds(q, 256, stride=8), :].T for q in range(8)], axis=0)
    high, low = split(turned)
    both = dot(jnp.concatenate([high, high, low], axis=1), y_ref[...])
    for q in range(8):
        cos, sin = both[128 * q : 128 * q + 128, :256], both[128 * q : 128 * q + 128, 256:]
        high, low = split(jnp.concatenate([cos * tr + sin * ti, sin * tr - cos * ti], axis=0))
        modes = dot(last_ref[...], jnp.concatenate([high, high, low], axis=0))
        sr, si, pr, pi = modes[:32], modes[32:64], modes[64:96], modes[96:]
        square = sr * sr + si * si
        some = square > 1e-30
        scale = lax.rsqrt(jnp.maximum(square, 1e-30))
        results = (
            square * scale,
            jnp.where(some, (sr * pr + si * pi) * scale, jnp.sqrt(pr * pr + pi * pi)),
            jnp.where(some, (si * pr - sr * pi) * scale, 0.0),
        )
        for o, result in enumerate(results):
            for p in range(2):
                for half in range(2):
                    block = result[16 * p : 16 * p + 16, 128 * half : 128 * half + 128]
                    out_ref[pl.ds(place(o, p, half, q), 16, stride=96), :] = block


def place(o, p, half, q):
    return 32 * o + 16 * p + 8 * half + q


def spectra_kernel(in_ref, out_ref, held, sems):
    factor = 64.0 / (4096 * 2048)
    row = lax.broadcasted_iota(jnp.int32, (128, 128), 0)
    col = lax.broadcasted_iota(jnp.int32, (128, 128), 1)
    device = lax.axis_index("gy") + lax.axis_index("gz")
    drop = row + col + device == 0
    copies = []
    for p in range(2):
        for half in range(2):
            at = 2 * p + half
            size, re, im = [
                jnp.concatenate([in_ref[pl.ds(place(o, p, half, q), 16, stride=96), :] for q in range(8)], axis=0).T
                for o in range(3)
            ]
            scaled = size * factor
            results = (size * scaled, (re * re + im * im) * factor, scaled * re, scaled * im)
            for o, result in enumerate(results):
                held[at, o] = jnp.where(drop, 0.0, result) if half == 0 else result
            copies.append(pltpu.make_async_copy(held.at[at], out_ref.at[:, p, pl.ds(128 * half, 128), :], sems.at[at]))
            copies[-1].start()
    for copy in copies:
        copy.wait()


def shape(*sizes):
    return jax.ShapeDtypeStruct(sizes, jnp.float32)


def shards(labels, porosity):
    count = lax.axis_size("gy")
    following = lax.ppermute(labels[:, :4, :], "gy", [((i + 1) % count, i) for i in range(count)])
    planes, ends, table = pl.pallas_call(
        planes_kernel,
        out_shape=(shape(16, 72, 128), shape(4, 24, 128), shape(8, 128)),
        in_specs=[HBM, HBM],
        out_specs=(VMEM, VMEM, VMEM),
        scratch_shapes=[
            pltpu.VMEM((6, 256, 128), jnp.int32),
            pltpu.SMEM((6,), jnp.float32),
            pltpu.VMEM((4, 256, 128), jnp.float32),
            pltpu.SemaphoreType.DMA((BLOCKS + 1,)),
        ],
        compiler_params=WIDE,
        cost_estimate=pl.CostEstimate(flops=10_000_000, bytes_accessed=4_000_000, transcendentals=0),
        name="planes",
    )(porosity, labels)
    rows = pl.pallas_call(
        rows_kernel,
        out_shape=shape(16, 72, 128),
        in_specs=[VMEM, VMEM, VMEM, VMEM],
        out_specs=VMEM,
        scratch_shapes=[pltpu.VMEM((4, 32, 128), jnp.float32)],
        compiler_params=PARAMS,
        name="rows",
    )(planes, ends, table, following)
    rows = lax.all_to_all(rows, "gz", 0, 0, tiled=True)
    columns = pl.pallas_call(
        columns_kernel,
        out_shape=shape(16, 128, 128),
        in_specs=[VMEM, VMEM],
        out_specs=VMEM,
        scratch_shapes=[pltpu.VMEM((16, 32, 128), jnp.float32), pltpu.VMEM((16, 64, 128), jnp.float32)],
        compiler_params=PARAMS,
        name="columns",
    )(rows, jnp.asarray(z_matrices()))
    columns = lax.all_to_all(columns.reshape(256, 8, 128), ("gy", "gz"), 0, 0, tiled=True)
    cos, sin = twiddles()
    modes = pl.pallas_call(
        modes_kernel,
        out_shape=shape(16 * 96, 128),
        in_specs=[VMEM] * 5,
        out_specs=VMEM,
        compiler_params=PARAMS,
        name="modes",
    )(columns.reshape(2048, 128), jnp.asarray(y_matrix()), jnp.asarray(cos), jnp.asarray(sin), jnp.asarray(last_matrix()))
    modes = lax.all_to_all(modes.reshape(16, 96, 128), "gy", 0, 0, tiled=True)
    return pl.pallas_call(
        spectra_kernel,
        out_shape=shape(4, 2, 256, 128),
        in_specs=[VMEM],
        out_specs=HBM,
        scratch_shapes=[pltpu.VMEM((4, 4, 128, 128), jnp.float32), pltpu.SemaphoreType.DMA((4,))],
        compiler_params=PARAMS,
        name="spectra",
    )(modes.reshape(16 * 96, 128))


def solution(mesh):
    placed = (P(None, "gy", "gz"), P())
    return jax.shard_map(
        shards, mesh=mesh, in_specs=placed, out_specs=P(None, None, "gy", "gz"), check_vma=False
    )
```

```python
import functools
import math

import jax
import jax.numpy as jnp
import ml_dtypes
import numpy as np
from jax import lax
from jax.experimental import pallas as pl
from jax.experimental.pallas import tpu as pltpu
from jax.sharding import PartitionSpec as P

VMEM = pl.BlockSpec(memory_space=pltpu.VMEM)
HBM = pl.BlockSpec(memory_space=pltpu.HBM)
PARAMS = pltpu.CompilerParams(vmem_limit_bytes=48 * 1024 * 1024)


def halves(matrix):
    high = matrix.astype(ml_dtypes.bfloat16)
    low = (matrix - high.astype(np.float64)).astype(ml_dtypes.bfloat16)
    return high, low


def split(value):
    high = value.astype(jnp.bfloat16)
    low = (value - high.astype(jnp.float32)).astype(jnp.bfloat16)
    return high, low


def dot(a, b):
    return lax.dot_general(a, b, (((1,), (0,)), ((), ())), preferred_element_type=jnp.float32)


def dot_t(a, b):
    return lax.dot_general(a, b, (((1,), (1,)), ((), ())), preferred_element_type=jnp.float32)


def joined(matrix, axis):
    high, low = halves(matrix)
    return np.concatenate([high, low, high], axis=axis)


def z_matrices():
    q = np.arange(128)[:, None]
    j = np.arange(128)[None, :]
    angles = [2.0 * math.pi / 2048 * ((j * (16 * q + s)) % 2048) for s in range(9)]
    return np.stack([joined(np.concatenate([np.cos(t), np.sin(t)], axis=1), 1) for t in angles])


def y_matrix():
    i = np.arange(256)[:, None]
    m = np.arange(256)[None, :]
    theta = 2.0 * math.pi / 256 * ((i * m) % 256)
    return joined(np.concatenate([np.cos(theta), np.sin(theta)], axis=1), 0)


def twiddles():
    r = np.arange(128)[:, None] % 16
    m = np.arange(256)[None, :]
    phi = 2.0 * math.pi / 4096 * (m * r)
    return np.cos(phi).astype(np.float32), (-np.sin(phi)).astype(np.float32)


def last_matrix():
    w = np.zeros((4, 2, 16, 2, 2, 2, 2, 16))
    g = np.arange(16)[:, None]
    r = np.arange(16)[None, :]
    psi = 2.0 * math.pi / 16 * ((g * r) % 16)
    cos, sin = np.cos(psi), np.sin(psi)
    for field in range(2):
        for plane in range(2):
            w[2 * field, plane, :, 0, 0, field, plane] = cos
            w[2 * field, plane, :, 1, 1, field, plane] = cos
            w[2 * field, plane, :, 0, 1, field, plane] = sin
            w[2 * field, plane, :, 1, 0, field, plane] = -sin
            w[2 * field + 1, plane, :, 0, 1, field, plane] = cos
            w[2 * field + 1, plane, :, 1, 0, field, plane] = -cos
            w[2 * field + 1, plane, :, 0, 0, field, plane] = -sin
            w[2 * field + 1, plane, :, 1, 1, field, plane] = -sin
    return joined(w.reshape(128, 256), 1)


def fill(values, ids):
    value = jnp.where(ids == 1, values[1], values[0])
    for k in range(2, 6):
        value = jnp.where(ids == k, values[k], value)
    return value


def along_x(f):
    s = [(f[k] + 6.0 * f[k + 1] + f[k + 2]) * 0.125 for k in range(4)]
    return [s[2] - s[0], s[3] - s[1], s[1], s[2]]


def along_y(ext, a, first, count):
    return (
        ext[a, first + 1 : first + 1 + count, :]
        + 6.0 * ext[a, first + 2 : first + 2 + count, :]
        + ext[a, first + 3 : first + 3 + count, :]
    ) * 0.125


BLOCKS = 4
TALL = 256 // BLOCKS


def planes_kernel(por_ref, lab_ref, out_ref, end_ref, table_ref, held, few, ext, sems):
    copies = [pltpu.make_async_copy(por_ref, few, sems.at[BLOCKS])]
    for b in range(BLOCKS):
        rows = pl.ds(TALL * b, TALL)
        copies.append(pltpu.make_async_copy(lab_ref.at[:, rows, :], held.at[:, rows, :], sems.at[b]))
    for copy in copies:
        copy.start()
    copies[0].wait()
    values = [few[k] for k in range(6)]
    for k in range(6):
        table_ref[k : k + 1, :] = jnp.full((1, 128), values[k], jnp.float32)
    table_ref[6:8, :] = jnp.zeros((2, 128), jnp.float32)
    done = 0
    for b in range(BLOCKS):
        copies[1 + b].wait()
        rows = pl.ds(TALL * b, TALL)
        for a, value in enumerate(along_x([fill(values, held[x, rows, :]) for x in range(6)])):
            ext[a, rows, :] = value
        ready = (TALL * (b + 1) - 3) // 16
        for a in range(4):
            block = along_y(ext, a, 16 * done, 16 * (ready - done))
            out_ref[done:ready, 16 * a : 16 * a + 16, :] = block.reshape(ready - done, 16, 128)
        done = ready
    for p in range(2):
        a = 2 + p
        for d in range(15):
            below = along_y(ext, a, -1, 1) if d == 0 else out_ref[d - 1, 16 * a + 15 : 16 * a + 16, :]
            above = along_y(ext, a, 240, 1) if d == 14 else out_ref[d + 1, 16 * a : 16 * a + 1, :]
            out_ref[d, 64 + 2 * p : 65 + 2 * p, :] = below
            out_ref[d, 65 + 2 * p : 66 + 2 * p, :] = above
    out_ref[0:15, 68:72, :] = jnp.zeros((15, 4, 128), jnp.float32)
    out_ref[15] = jnp.zeros((72, 128), jnp.float32)
    end_ref[...] = ext[:, 232:256, :]


def rows_kernel(in_ref, end_ref, table_ref, next_ref, out_ref, ext):
    out_ref[0:15] = in_ref[0:15]
    ext[:, 0:24, :] = end_ref[...]
    values = [table_ref[k : k + 1, :] for k in range(6)]
    for a, value in enumerate(along_x([fill(values, next_ref[x]) for x in range(6)])):
        ext[a, 24:28, :] = value
        out_ref[15, 16 * a : 16 * a + 16, :] = along_y(ext, a, 8, 16)
    for p in range(2):
        a = 2 + p
        out_ref[15, 64 + 2 * p : 65 + 2 * p, :] = along_y(ext, a, 7, 1)
        out_ref[15, 65 + 2 * p : 66 + 2 * p, :] = along_y(ext, a, 24, 1)
    out_ref[15, 68:72, :] = jnp.zeros((4, 128), jnp.float32)


def real_transform(x):
    n = len(x)
    if n == 2:
        return [(x[0] + x[1], None), (x[0] - x[1], None)]
    even = real_transform(x[0::2])
    odd = real_transform(x[1::2])
    out = [None] * (n // 2 + 1)
    for k in range(n // 4 + 1):
        (er, ei), (dr, di) = even[k], odd[k]
        c, s = math.cos(2.0 * math.pi * k / n), math.sin(2.0 * math.pi * k / n)
        if k == 0:
            out[0] = (er + dr, None)
            out[n // 2] = (er - dr, None)
        elif 4 * k == n:
            out[k] = (er, -dr)
        else:
            tr = c * dr if di is None else c * dr + s * di
            ti = -s * dr if di is None else c * di - s * dr
            out[k] = (er + tr, ti if ei is None else ei + ti)
            out[n // 2 - k] = (er - tr, ti if ei is None else ti - ei)
    return out


def columns_kernel(in_ref, w_ref, out_ref, ext, x_ref):
    lane = lax.broadcasted_iota(jnp.int32, (16, 16, 128), 2)

    def before(x):
        rolled = pltpu.roll(x, 1, 2)
        return jnp.where(lane == 0, jnp.concatenate([rolled[15:], rolled[:15]], axis=0), rolled)

    def after(x):
        rolled = pltpu.roll(x, 127, 2)
        return jnp.where(lane == 127, jnp.concatenate([rolled[1:], rolled[:1]], axis=0), rolled)

    def along_z(x):
        return (before(x) + 6.0 * x + after(x)) * 0.125

    for p in range(2):
        center = in_ref[:, 32 + 16 * p : 48 + 16 * p, :]
        ext[:, 8:24, :] = center
        ext[:, 7:8, :] = in_ref[:, 64 + 2 * p : 65 + 2 * p, :]
        ext[:, 24:25, :] = in_ref[:, 65 + 2 * p : 66 + 2 * p, :]
        grad_x = along_z(in_ref[:, 16 * p : 16 * p + 16, :])
        grad_y = along_z(ext[:, 9:25, :] - ext[:, 7:23, :])
        pore = along_z(center)
        grad_z = after(pore) - before(pore)
        surface = jnp.sqrt(grad_x * grad_x + grad_y * grad_y + grad_z * grad_z + 0.01)
        x_ref[:, 16 * p : 16 * p + 16, :] = surface
        x_ref[:, 32 + 16 * p : 48 + 16 * p, :] = pore
    parts = real_transform([x_ref[d] for d in range(16)])
    sign = jnp.where(lax.broadcasted_iota(jnp.int32, (128, 128), 1) < 64, 1.0, -1.0)

    def arranged(k):
        re, im = parts[k]
        if im is None:
            im = jnp.zeros_like(re)
        top = jnp.concatenate([re, im], axis=1)
        bottom = jnp.concatenate([im, -re], axis=1)
        high, low = split(jnp.concatenate([top, bottom], axis=0))
        return jnp.concatenate([high, high, low], axis=1)

    for k in range(9):
        wave = dot_t(w_ref[k], arranged(k))
        out_ref[k] = wave
        if 0 < k < 8:
            wave = wave * sign
            for block in range(16):
                out_ref[16 - k, 8 * block : 8 * block + 8, :] = wave[120 - 8 * block : 128 - 8 * block]


def modes_kernel(in_ref, y_ref, tr_ref, ti_ref, last_ref, out_ref):
    tr, ti = tr_ref[...], ti_ref[...]
    backwards = lax.axis_index("gy") > 8
    starts = [jnp.where(backwards, 7 - q, q) for q in range(8)]
    turned = jnp.concatenate([in_ref[pl.ds(start, 256, stride=8), :].T for start in starts], axis=0)
    high, low = split(turned)
    both = dot(jnp.concatenate([high, high, low], axis=1), y_ref[...])
    for q in range(8):
        cos, sin = both[128 * q : 128 * q + 128, :256], both[128 * q : 128 * q + 128, 256:]
        high, low = split(jnp.concatenate([cos * tr + sin * ti, sin * tr - cos * ti], axis=0))
        modes = dot(last_ref[...], jnp.concatenate([high, high, low], axis=0))
        sr, si, pr, pi = modes[:32], modes[32:64], modes[64:96], modes[96:]
        square = sr * sr + si * si
        some = square > 1e-30
        scale = lax.rsqrt(jnp.maximum(square, 1e-30))
        results = (
            square * scale,
            jnp.where(some, (sr * pr + si * pi) * scale, jnp.sqrt(pr * pr + pi * pi)),
            jnp.where(some, (si * pr - sr * pi) * scale, 0.0),
        )
        for o, result in enumerate(results):
            for p in range(2):
                for half in range(2):
                    block = result[16 * p : 16 * p + 16, 128 * half : 128 * half + 128]
                    out_ref[pl.ds(place(o, p, half, q), 16, stride=96), :] = block


def place(o, p, half, q):
    return 32 * o + 16 * p + 8 * half + q


def spectra_kernel(in_ref, out_ref, held, sems):
    factor = 64.0 / (4096 * 2048)
    row = lax.broadcasted_iota(jnp.int32, (128, 128), 0)
    col = lax.broadcasted_iota(jnp.int32, (128, 128), 1)
    device = lax.axis_index("gy") + lax.axis_index("gz")
    drop = row + col + device == 0
    copies = []
    for p in range(2):
        for half in range(2):
            at = 2 * p + half
            size, re, im = [
                jnp.concatenate([in_ref[pl.ds(place(o, p, half, q), 16, stride=96), :] for q in range(8)], axis=0).T
                for o in range(3)
            ]
            scaled = size * factor
            results = (size * scaled, (re * re + im * im) * factor, scaled * re, scaled * im)
            for o, result in enumerate(results):
                held[at, o] = jnp.where(drop, 0.0, result) if half == 0 else result
            copies.append(pltpu.make_async_copy(held.at[at], out_ref.at[:, p, pl.ds(128 * half, 128), :], sems.at[at]))
            copies[-1].start()
    for copy in copies:
        copy.wait()


def shape(*sizes):
    return jax.ShapeDtypeStruct(sizes, jnp.float32)


def shards(labels, porosity):
    count = lax.axis_size("gy")
    following = lax.ppermute(labels[:, :4, :], "gy", [((i + 1) % count, i) for i in range(count)])
    planes, ends, table = pl.pallas_call(
        planes_kernel,
        out_shape=(shape(16, 72, 128), shape(4, 24, 128), shape(8, 128)),
        in_specs=[HBM, HBM],
        out_specs=(VMEM, VMEM, VMEM),
        scratch_shapes=[
            pltpu.VMEM((6, 256, 128), jnp.int32),
            pltpu.SMEM((6,), jnp.float32),
            pltpu.VMEM((4, 256, 128), jnp.float32),
            pltpu.SemaphoreType.DMA((BLOCKS + 1,)),
        ],
        compiler_params=PARAMS,
        cost_estimate=pl.CostEstimate(flops=10_000_000, bytes_accessed=4_000_000, transcendentals=0),
        name="planes",
    )(*[pltpu.with_memory_space_constraint(array, pltpu.HBM) for array in (porosity, labels)])
    rows = pl.pallas_call(
        rows_kernel,
        out_shape=shape(16, 72, 128),
        in_specs=[VMEM, VMEM, VMEM, VMEM],
        out_specs=VMEM,
        scratch_shapes=[pltpu.VMEM((4, 32, 128), jnp.float32)],
        compiler_params=PARAMS,
        name="rows",
    )(planes, ends, table, following)
    rows = lax.all_to_all(rows, "gz", 0, 0, tiled=True)
    columns = pl.pallas_call(
        columns_kernel,
        out_shape=shape(16, 128, 128),
        in_specs=[VMEM, VMEM],
        out_specs=VMEM,
        scratch_shapes=[pltpu.VMEM((16, 32, 128), jnp.float32), pltpu.VMEM((16, 64, 128), jnp.float32)],
        compiler_params=PARAMS,
        name="columns",
    )(rows, jnp.asarray(z_matrices()))
    columns = lax.all_to_all(columns.reshape(256, 8, 128), ("gy", "gz"), 0, 0, tiled=True)
    cos, sin = twiddles()
    modes = pl.pallas_call(
        modes_kernel,
        out_shape=shape(16 * 96, 128),
        in_specs=[VMEM] * 5,
        out_specs=VMEM,
        compiler_params=PARAMS,
        name="modes",
    )(columns.reshape(2048, 128), jnp.asarray(y_matrix()), jnp.asarray(cos), jnp.asarray(sin), jnp.asarray(last_matrix()))
    modes = lax.all_to_all(modes.reshape(16, 96, 128), "gy", 0, 0, tiled=True)
    return pl.pallas_call(
        spectra_kernel,
        out_shape=shape(4, 2, 256, 128),
        in_specs=[VMEM],
        out_specs=HBM,
        scratch_shapes=[pltpu.VMEM((4, 4, 128, 128), jnp.float32), pltpu.SemaphoreType.DMA((4,))],
        compiler_params=PARAMS,
        name="spectra",
    )(modes.reshape(16 * 96, 128))


def solution(mesh):
    placed = (P(None, "gy", "gz"), P())
    return jax.shard_map(
        shards, mesh=mesh, in_specs=placed, out_specs=P(None, None, "gy", "gz"), check_vma=False
    )
```

```python
import functools
import math

import jax
import jax.numpy as jnp
import ml_dtypes
import numpy as np
from jax import lax
from jax.experimental import pallas as pl
from jax.experimental.pallas import tpu as pltpu
from jax.sharding import PartitionSpec as P

VMEM = pl.BlockSpec(memory_space=pltpu.VMEM)
HBM = pl.BlockSpec(memory_space=pltpu.HBM)
PARAMS = pltpu.CompilerParams(vmem_limit_bytes=48 * 1024 * 1024)


def halves(matrix):
    high = matrix.astype(ml_dtypes.bfloat16)
    low = (matrix - high.astype(np.float64)).astype(ml_dtypes.bfloat16)
    return high, low


def split(value):
    high = value.astype(jnp.bfloat16)
    low = (value - high.astype(jnp.float32)).astype(jnp.bfloat16)
    return high, low


def dot(a, b):
    return lax.dot_general(a, b, (((1,), (0,)), ((), ())), preferred_element_type=jnp.float32)


def dot_t(a, b):
    return lax.dot_general(a, b, (((1,), (1,)), ((), ())), preferred_element_type=jnp.float32)


def joined(matrix, axis):
    high, low = halves(matrix)
    return np.concatenate([high, low, high], axis=axis)


def z_matrices():
    q = np.arange(128)[:, None]
    j = np.arange(128)[None, :]
    angles = [2.0 * math.pi / 2048 * ((j * (16 * q + s)) % 2048) for s in range(9)]
    return np.stack([joined(np.concatenate([np.cos(t), np.sin(t)], axis=1), 1) for t in angles])


def y_matrix():
    i = np.arange(256)[:, None]
    m = np.arange(256)[None, :]
    theta = 2.0 * math.pi / 256 * ((i * m) % 256)
    return joined(np.concatenate([np.cos(theta), np.sin(theta)], axis=1), 0)


def twiddles():
    r = np.arange(128)[:, None] % 16
    m = np.arange(256)[None, :]
    phi = 2.0 * math.pi / 4096 * (m * r)
    return np.cos(phi).astype(np.float32), (-np.sin(phi)).astype(np.float32)


def last_matrix():
    w = np.zeros((4, 2, 16, 2, 2, 2, 2, 16))
    g = np.arange(16)[:, None]
    r = np.arange(16)[None, :]
    psi = 2.0 * math.pi / 16 * ((g * r) % 16)
    cos, sin = np.cos(psi), np.sin(psi)
    for field in range(2):
        for plane in range(2):
            w[2 * field, plane, :, 0, 0, field, plane] = cos
            w[2 * field, plane, :, 1, 1, field, plane] = cos
            w[2 * field, plane, :, 0, 1, field, plane] = sin
            w[2 * field, plane, :, 1, 0, field, plane] = -sin
            w[2 * field + 1, plane, :, 0, 1, field, plane] = cos
            w[2 * field + 1, plane, :, 1, 0, field, plane] = -cos
            w[2 * field + 1, plane, :, 0, 0, field, plane] = -sin
            w[2 * field + 1, plane, :, 1, 1, field, plane] = -sin
    return joined(w.reshape(128, 256), 1)


def fill(values, ids):
    value = jnp.where(ids == 1, values[1], values[0])
    for k in range(2, 6):
        value = jnp.where(ids == k, values[k], value)
    return value


def along_x(f):
    s = [(f[k] + 6.0 * f[k + 1] + f[k + 2]) * 0.125 for k in range(4)]
    return [s[2] - s[0], s[3] - s[1], s[1], s[2]]


def along_y(ext, a, first, count):
    return (
        ext[a, first + 1 : first + 1 + count, :]
        + 6.0 * ext[a, first + 2 : first + 2 + count, :]
        + ext[a, first + 3 : first + 3 + count, :]
    ) * 0.125


CHUNK = 68
BLOCKS = 4
TALL = 256 // BLOCKS


def planes_kernel(por_ref, lab_ref, out_ref, end_ref, table_ref, held, few, ext, sems):
    copies = [pltpu.make_async_copy(por_ref, few, sems.at[BLOCKS])]
    for b in range(BLOCKS):
        rows = pl.ds(TALL * b, TALL)
        copies.append(pltpu.make_async_copy(lab_ref.at[:, rows, :], held.at[:, rows, :], sems.at[b]))
    for copy in copies:
        copy.start()
    copies[0].wait()
    values = [few[k] for k in range(6)]
    for k in range(6):
        table_ref[k : k + 1, :] = jnp.full((1, 128), values[k], jnp.float32)
    table_ref[6:8, :] = jnp.zeros((2, 128), jnp.float32)
    done = 0
    for b in range(BLOCKS):
        copies[1 + b].wait()
        rows = pl.ds(TALL * b, TALL)
        for a, value in enumerate(along_x([fill(values, held[x, rows, :]) for x in range(6)])):
            ext[a, rows, :] = value
        ready = (TALL * (b + 1) - 3) // 16
        for a in range(4):
            for d in range(done, ready):
                at = CHUNK * d + 16 * a
                out_ref[at : at + 16, :] = along_y(ext, a, 16 * d, 16)
        done = ready
    for p in range(2):
        a = 2 + p
        for d in range(15):
            at = CHUNK * d + 16 * a
            edge = CHUNK * d + 64 + 2 * p
            below = along_y(ext, a, -1, 1) if d == 0 else out_ref[at - CHUNK + 15 : at - CHUNK + 16, :]
            above = along_y(ext, a, 240, 1) if d == 14 else out_ref[at + CHUNK : at + CHUNK + 1, :]
            out_ref[edge : edge + 1, :] = below
            out_ref[edge + 1 : edge + 2, :] = above
    out_ref[15 * CHUNK :, :] = jnp.zeros((CHUNK, 128), jnp.float32)
    end_ref[...] = ext[:, 232:256, :]


def rows_kernel(in_ref, end_ref, table_ref, next_ref, out_ref, ext):
    last = 15 * CHUNK
    out_ref[:last, :] = in_ref[:last, :]
    ext[:, 0:24, :] = end_ref[...]
    values = [table_ref[k : k + 1, :] for k in range(6)]
    for a, value in enumerate(along_x([fill(values, next_ref[x]) for x in range(6)])):
        ext[a, 24:28, :] = value
        out_ref[last + 16 * a : last + 16 * a + 16, :] = along_y(ext, a, 8, 16)
    for p in range(2):
        a = 2 + p
        edge = last + 64 + 2 * p
        out_ref[edge : edge + 1, :] = along_y(ext, a, 7, 1)
        out_ref[edge + 1 : edge + 2, :] = along_y(ext, a, 24, 1)


def real_transform(x):
    n = len(x)
    if n == 2:
        return [(x[0] + x[1], None), (x[0] - x[1], None)]
    even = real_transform(x[0::2])
    odd = real_transform(x[1::2])
    out = [None] * (n // 2 + 1)
    for k in range(n // 4 + 1):
        (er, ei), (dr, di) = even[k], odd[k]
        c, s = math.cos(2.0 * math.pi * k / n), math.sin(2.0 * math.pi * k / n)
        if k == 0:
            out[0] = (er + dr, None)
            out[n // 2] = (er - dr, None)
        elif 4 * k == n:
            out[k] = (er, -dr)
        else:
            tr = c * dr if di is None else c * dr + s * di
            ti = -s * dr if di is None else c * di - s * dr
            out[k] = (er + tr, ti if ei is None else ei + ti)
            out[n // 2 - k] = (er - tr, ti if ei is None else ti - ei)
    return out


def columns_kernel(in_ref, w_ref, out_ref, ext, x_ref):
    lane = lax.broadcasted_iota(jnp.int32, (16, 16, 128), 2)

    def before(x):
        rolled = pltpu.roll(x, 1, 2)
        return jnp.where(lane == 0, jnp.concatenate([rolled[15:], rolled[:15]], axis=0), rolled)

    def after(x):
        rolled = pltpu.roll(x, 127, 2)
        return jnp.where(lane == 127, jnp.concatenate([rolled[1:], rolled[:1]], axis=0), rolled)

    def along_z(x):
        return (before(x) + 6.0 * x + after(x)) * 0.125

    def rows(first, count):
        return jnp.stack([in_ref[CHUNK * d + first : CHUNK * d + first + count, :] for d in range(16)])

    for p in range(2):
        center = rows(32 + 16 * p, 16)
        ext[:, 8:24, :] = center
        ext[:, 7:8, :] = rows(64 + 2 * p, 1)
        ext[:, 24:25, :] = rows(65 + 2 * p, 1)
        grad_x = along_z(rows(16 * p, 16))
        grad_y = along_z(ext[:, 9:25, :] - ext[:, 7:23, :])
        pore = along_z(center)
        grad_z = after(pore) - before(pore)
        surface = jnp.sqrt(grad_x * grad_x + grad_y * grad_y + grad_z * grad_z + 0.01)
        x_ref[:, 16 * p : 16 * p + 16, :] = surface
        x_ref[:, 32 + 16 * p : 48 + 16 * p, :] = pore
    parts = real_transform([x_ref[d] for d in range(16)])
    sign = jnp.where(lax.broadcasted_iota(jnp.int32, (128, 128), 1) < 64, 1.0, -1.0)

    def arranged(k):
        re, im = parts[k]
        if im is None:
            im = jnp.zeros_like(re)
        top = jnp.concatenate([re, im], axis=1)
        bottom = jnp.concatenate([im, -re], axis=1)
        high, low = split(jnp.concatenate([top, bottom], axis=0))
        return jnp.concatenate([high, high, low], axis=1)

    for k in range(9):
        wave = dot_t(w_ref[k], arranged(k))
        out_ref[k] = wave
        if 0 < k < 8:
            wave = wave * sign
            for block in range(16):
                out_ref[16 - k, 8 * block : 8 * block + 8, :] = wave[120 - 8 * block : 128 - 8 * block]


def modes_kernel(in_ref, y_ref, tr_ref, ti_ref, last_ref, out_ref):
    tr, ti = tr_ref[...], ti_ref[...]
    backwards = lax.axis_index("gy") > 8
    starts = [jnp.where(backwards, 7 - q, q) for q in range(8)]
    turned = jnp.concatenate([in_ref[pl.ds(start, 256, stride=8), :].T for start in starts], axis=0)
    high, low = split(turned)
    both = dot(jnp.concatenate([high, high, low], axis=1), y_ref[...])
    for q in range(8):
        cos, sin = both[128 * q : 128 * q + 128, :256], both[128 * q : 128 * q + 128, 256:]
        high, low = split(jnp.concatenate([cos * tr + sin * ti, sin * tr - cos * ti], axis=0))
        modes = dot(last_ref[...], jnp.concatenate([high, high, low], axis=0))
        sr, si, pr, pi = modes[:32], modes[32:64], modes[64:96], modes[96:]
        square = sr * sr + si * si
        some = square > 1e-30
        scale = lax.rsqrt(jnp.maximum(square, 1e-30))
        results = (
            square * scale,
            jnp.where(some, (sr * pr + si * pi) * scale, jnp.sqrt(pr * pr + pi * pi)),
            jnp.where(some, (si * pr - sr * pi) * scale, 0.0),
        )
        for o, result in enumerate(results):
            for p in range(2):
                for half in range(2):
                    block = result[16 * p : 16 * p + 16, 128 * half : 128 * half + 128]
                    out_ref[pl.ds(place(o, p, half, q), 16, stride=96), :] = block


def place(o, p, half, q):
    return 32 * o + 16 * p + 8 * half + q


def spectra_kernel(in_ref, out_ref, held, sems):
    factor = 64.0 / (4096 * 2048)
    row = lax.broadcasted_iota(jnp.int32, (128, 128), 0)
    col = lax.broadcasted_iota(jnp.int32, (128, 128), 1)
    device = lax.axis_index("gy") + lax.axis_index("gz")
    drop = row + col + device == 0
    copies = []
    for p in range(2):
        for half in range(2):
            at = 2 * p + half
            size, re, im = [
                jnp.concatenate([in_ref[pl.ds(place(o, p, half, q), 16, stride=96), :] for q in range(8)], axis=0).T
                for o in range(3)
            ]
            scaled = size * factor
            results = (size * scaled, (re * re + im * im) * factor, scaled * re, scaled * im)
            for o, result in enumerate(results):
                held[at, o] = jnp.where(drop, 0.0, result) if half == 0 else result
            copies.append(pltpu.make_async_copy(held.at[at], out_ref.at[:, p, pl.ds(128 * half, 128), :], sems.at[at]))
            copies[-1].start()
    for copy in copies:
        copy.wait()


def shape(*sizes):
    return jax.ShapeDtypeStruct(sizes, jnp.float32)


def shards(labels, porosity):
    count = lax.axis_size("gy")
    following = lax.ppermute(labels[:, :4, :], "gy", [((i + 1) % count, i) for i in range(count)])
    planes, ends, table = pl.pallas_call(
        planes_kernel,
        out_shape=(shape(16 * CHUNK, 128), shape(4, 24, 128), shape(8, 128)),
        in_specs=[HBM, HBM],
        out_specs=(VMEM, VMEM, VMEM),
        scratch_shapes=[
            pltpu.VMEM((6, 256, 128), jnp.int32),
            pltpu.SMEM((6,), jnp.float32),
            pltpu.VMEM((4, 256, 128), jnp.float32),
            pltpu.SemaphoreType.DMA((BLOCKS + 1,)),
        ],
        compiler_params=PARAMS,
        cost_estimate=pl.CostEstimate(flops=10_000_000, bytes_accessed=4_000_000, transcendentals=0),
        name="planes",
    )(*[pltpu.with_memory_space_constraint(array, pltpu.HBM) for array in (porosity, labels)])
    rows = pl.pallas_call(
        rows_kernel,
        out_shape=shape(16 * CHUNK, 128),
        in_specs=[VMEM, VMEM, VMEM, VMEM],
        out_specs=VMEM,
        scratch_shapes=[pltpu.VMEM((4, 32, 128), jnp.float32)],
        compiler_params=PARAMS,
        name="rows",
    )(planes, ends, table, following)
    rows = lax.all_to_all(rows.reshape(4 * CHUNK, 4, 128), "gz", 0, 0, tiled=True).reshape(16 * CHUNK, 128)
    columns = pl.pallas_call(
        columns_kernel,
        out_shape=shape(16, 128, 128),
        in_specs=[VMEM, VMEM],
        out_specs=VMEM,
        scratch_shapes=[pltpu.VMEM((16, 32, 128), jnp.float32), pltpu.VMEM((16, 64, 128), jnp.float32)],
        compiler_params=PARAMS,
        name="columns",
    )(rows, jnp.asarray(z_matrices()))
    columns = lax.all_to_all(columns.reshape(256, 8, 128), ("gy", "gz"), 0, 0, tiled=True)
    cos, sin = twiddles()
    modes = pl.pallas_call(
        modes_kernel,
        out_shape=shape(16 * 96, 128),
        in_specs=[VMEM] * 5,
        out_specs=VMEM,
        compiler_params=PARAMS,
        name="modes",
    )(columns.reshape(2048, 128), jnp.asarray(y_matrix()), jnp.asarray(cos), jnp.asarray(sin), jnp.asarray(last_matrix()))
    modes = lax.all_to_all(modes.reshape(16, 96, 128), "gy", 0, 0, tiled=True)
    return pl.pallas_call(
        spectra_kernel,
        out_shape=shape(4, 2, 256, 128),
        in_specs=[VMEM],
        out_specs=HBM,
        scratch_shapes=[pltpu.VMEM((4, 4, 128, 128), jnp.float32), pltpu.SemaphoreType.DMA((4,))],
        compiler_params=PARAMS,
        name="spectra",
    )(modes.reshape(16 * 96, 128))


def solution(mesh):
    placed = (P(None, "gy", "gz"), P())
    return jax.shard_map(
        shards, mesh=mesh, in_specs=placed, out_specs=P(None, None, "gy", "gz"), check_vma=False
    )
```

```python
import functools
import math

import jax
import jax.numpy as jnp
import ml_dtypes
import numpy as np
from jax import lax
from jax.experimental import pallas as pl
from jax.experimental.pallas import tpu as pltpu
from jax.sharding import PartitionSpec as P

VMEM = pl.BlockSpec(memory_space=pltpu.VMEM)
HBM = pl.BlockSpec(memory_space=pltpu.HBM)
PARAMS = pltpu.CompilerParams(vmem_limit_bytes=48 * 1024 * 1024)


def halves(matrix):
    high = matrix.astype(ml_dtypes.bfloat16)
    low = (matrix - high.astype(np.float64)).astype(ml_dtypes.bfloat16)
    return high, low


def split(value):
    high = value.astype(jnp.bfloat16)
    low = (value - high.astype(jnp.float32)).astype(jnp.bfloat16)
    return high, low


def dot(a, b):
    return lax.dot_general(a, b, (((1,), (0,)), ((), ())), preferred_element_type=jnp.float32)


def dot_t(a, b):
    return lax.dot_general(a, b, (((1,), (1,)), ((), ())), preferred_element_type=jnp.float32)


def joined(matrix, axis):
    high, low = halves(matrix)
    return np.concatenate([high, low, high], axis=axis)


PAIRED = (1, 2, 3, 5, 6, 7, 9, 10, 11, 13, 14, 15)
SINGLE = (0, 4, 8, 12)
DOUBLES = (1, 2, 3, 5, 6, 7)


def z_matrices():
    j = np.arange(128)[None, :]

    def block(s, count):
        theta = 2.0 * math.pi / 2048 * ((j * (16 * np.arange(count)[:, None] + s)) % 2048)
        return np.concatenate([np.cos(theta), np.sin(theta) * (1.0 if s <= 8 else -1.0)], axis=1)

    blocks = [block(s, 128) for s in (0, 8, 4, 12)]
    for k in DOUBLES:
        blocks += [block(k, 64), block(16 - k, 64)]
    return joined(np.concatenate(blocks, axis=0), 1)


def order_matrices():
    out = np.zeros((2, 4, 32, 128))
    for source in range(32):
        side, (i, b) = source // 16, divmod(source % 16, 2)
        combo = 2 * b + side
        for slot in range(3):
            t = 16 * i + PAIRED[3 * combo + slot]
            out[0, slot, source, t] = 1.0
            out[1, slot, source, 128 - t] = 1.0
        out[:, 3, source, 16 * i + SINGLE[combo]] = 1.0
    out = out.reshape(2, 128, 128)
    return np.concatenate([out, out], axis=1).astype(ml_dtypes.bfloat16)


def y_matrix():
    i = np.arange(256)[:, None]
    m = np.arange(256)[None, :]
    theta = 2.0 * math.pi / 256 * ((i * m) % 256)
    return joined(np.concatenate([np.cos(theta), np.sin(theta)], axis=1), 0)


def twiddles():
    r = np.arange(128)[:, None] % 16
    m = np.arange(256)[None, :]
    phi = 2.0 * math.pi / 4096 * (m * r)
    return np.cos(phi).astype(np.float32), (-np.sin(phi)).astype(np.float32)


def last_matrix():
    w = np.zeros((4, 2, 16, 2, 2, 2, 2, 16))
    g = np.arange(16)[:, None]
    r = np.arange(16)[None, :]
    psi = 2.0 * math.pi / 16 * ((g * r) % 16)
    cos, sin = np.cos(psi), np.sin(psi)
    for field in range(2):
        for plane in range(2):
            w[2 * field, plane, :, 0, 0, field, plane] = cos
            w[2 * field, plane, :, 1, 1, field, plane] = cos
            w[2 * field, plane, :, 0, 1, field, plane] = sin
            w[2 * field, plane, :, 1, 0, field, plane] = -sin
            w[2 * field + 1, plane, :, 0, 1, field, plane] = cos
            w[2 * field + 1, plane, :, 1, 0, field, plane] = -cos
            w[2 * field + 1, plane, :, 0, 0, field, plane] = -sin
            w[2 * field + 1, plane, :, 1, 1, field, plane] = -sin
    mirrored = w.copy()
    mirrored[:, :, :, :, 1] *= -1.0
    return joined(np.concatenate([w.reshape(128, 256), mirrored.reshape(128, 256)], axis=0), 1)


def fill(values, ids):
    value = jnp.where(ids == 1, values[1], values[0])
    for k in range(2, 6):
        value = jnp.where(ids == k, values[k], value)
    return value


def along_x(f):
    s = [(f[k] + 6.0 * f[k + 1] + f[k + 2]) * 0.125 for k in range(4)]
    return [s[2] - s[0], s[3] - s[1], s[1], s[2]]


def along_y(ext, a, first, count):
    return (
        ext[a, first + 1 : first + 1 + count, :]
        + 6.0 * ext[a, first + 2 : first + 2 + count, :]
        + ext[a, first + 3 : first + 3 + count, :]
    ) * 0.125


CHUNK = 68
BLOCKS = 4
TALL = 256 // BLOCKS


def planes_kernel(por_ref, lab_ref, out_ref, end_ref, table_ref, held, few, ext, sems):
    copies = [pltpu.make_async_copy(por_ref, few, sems.at[BLOCKS])]
    for b in range(BLOCKS):
        rows = pl.ds(TALL * b, TALL)
        copies.append(pltpu.make_async_copy(lab_ref.at[:, rows, :], held.at[:, rows, :], sems.at[b]))
    for copy in copies:
        copy.start()
    copies[0].wait()
    values = [few[k] for k in range(6)]
    for k in range(6):
        table_ref[k : k + 1, :] = jnp.full((1, 128), values[k], jnp.float32)
    table_ref[6:8, :] = jnp.zeros((2, 128), jnp.float32)
    done = 0
    for b in range(BLOCKS):
        copies[1 + b].wait()
        rows = pl.ds(TALL * b, TALL)
        for a, value in enumerate(along_x([fill(values, held[x, rows, :]) for x in range(6)])):
            ext[a, rows, :] = value
        ready = (TALL * (b + 1) - 3) // 16
        for a in range(4):
            for d in range(done, ready):
                at = CHUNK * d + 16 * a
                out_ref[at : at + 16, :] = along_y(ext, a, 16 * d, 16)
        done = ready
    for p in range(2):
        a = 2 + p
        for d in range(15):
            at = CHUNK * d + 16 * a
            edge = CHUNK * d + 64 + 2 * p
            below = along_y(ext, a, -1, 1) if d == 0 else out_ref[at - CHUNK + 15 : at - CHUNK + 16, :]
            above = along_y(ext, a, 240, 1) if d == 14 else out_ref[at + CHUNK : at + CHUNK + 1, :]
            out_ref[edge : edge + 1, :] = below
            out_ref[edge + 1 : edge + 2, :] = above
    out_ref[15 * CHUNK :, :] = jnp.zeros((CHUNK, 128), jnp.float32)
    end_ref[...] = ext[:, 232:256, :]


def rows_kernel(in_ref, end_ref, table_ref, next_ref, out_ref, ext):
    last = 15 * CHUNK
    out_ref[:last, :] = in_ref[:last, :]
    ext[:, 0:24, :] = end_ref[...]
    values = [table_ref[k : k + 1, :] for k in range(6)]
    for a, value in enumerate(along_x([fill(values, next_ref[x]) for x in range(6)])):
        ext[a, 24:28, :] = value
        out_ref[last + 16 * a : last + 16 * a + 16, :] = along_y(ext, a, 8, 16)
    for p in range(2):
        a = 2 + p
        edge = last + 64 + 2 * p
        out_ref[edge : edge + 1, :] = along_y(ext, a, 7, 1)
        out_ref[edge + 1 : edge + 2, :] = along_y(ext, a, 24, 1)


def real_transform(x):
    n = len(x)
    if n == 2:
        return [(x[0] + x[1], None), (x[0] - x[1], None)]
    even = real_transform(x[0::2])
    odd = real_transform(x[1::2])
    out = [None] * (n // 2 + 1)
    for k in range(n // 4 + 1):
        (er, ei), (dr, di) = even[k], odd[k]
        c, s = math.cos(2.0 * math.pi * k / n), math.sin(2.0 * math.pi * k / n)
        if k == 0:
            out[0] = (er + dr, None)
            out[n // 2] = (er - dr, None)
        elif 4 * k == n:
            out[k] = (er, -dr)
        else:
            tr = c * dr if di is None else c * dr + s * di
            ti = -s * dr if di is None else c * di - s * dr
            out[k] = (er + tr, ti if ei is None else ei + ti)
            out[n // 2 - k] = (er - tr, ti if ei is None else ti - ei)
    return out


def columns_kernel(in_ref, w_ref, out_ref, ext, x_ref):
    lane = lax.broadcasted_iota(jnp.int32, (16, 16, 128), 2)

    def before(x):
        rolled = pltpu.roll(x, 1, 2)
        return jnp.where(lane == 0, jnp.concatenate([rolled[15:], rolled[:15]], axis=0), rolled)

    def after(x):
        rolled = pltpu.roll(x, 127, 2)
        return jnp.where(lane == 127, jnp.concatenate([rolled[1:], rolled[:1]], axis=0), rolled)

    def along_z(x):
        return (before(x) + 6.0 * x + after(x)) * 0.125

    def rows(first, count):
        return jnp.stack([in_ref[CHUNK * d + first : CHUNK * d + first + count, :] for d in range(16)])

    for p in range(2):
        center = rows(32 + 16 * p, 16)
        ext[:, 8:24, :] = center
        ext[:, 7:8, :] = rows(64 + 2 * p, 1)
        ext[:, 24:25, :] = rows(65 + 2 * p, 1)
        grad_x = along_z(rows(16 * p, 16))
        grad_y = along_z(ext[:, 9:25, :] - ext[:, 7:23, :])
        pore = along_z(center)
        grad_z = after(pore) - before(pore)
        surface = jnp.sqrt(grad_x * grad_x + grad_y * grad_y + grad_z * grad_z + 0.01)
        x_ref[:, 16 * p : 16 * p + 16, :] = surface
        x_ref[:, 32 + 16 * p : 48 + 16 * p, :] = pore
    parts = real_transform([x_ref[d] for d in range(16)])
    sign = jnp.where(lax.broadcasted_iota(jnp.int32, (128, 128), 1) < 64, 1.0, -1.0)

    def arranged(k):
        re, im = parts[k]
        if im is None:
            im = jnp.zeros_like(re)
        top = jnp.concatenate([re, im], axis=1)
        bottom = jnp.concatenate([im, -re], axis=1)
        high, low = split(jnp.concatenate([top, bottom], axis=0))
        return jnp.concatenate([high, high, low], axis=1)

    def send(wave, s, blocks):
        paired = s in PAIRED
        combo, slot = divmod(PAIRED.index(s), 3) if paired else (SINGLE.index(s), 3)
        b, side = divmod(combo, 2)
        for block in range(blocks):
            low = min(block, 15 - block)
            gz = 15 - low if side else low
            at = 5 * (16 * b + gz) + slot + (1 if block > 7 else 0)
            out_ref[pl.ds(at, 8, stride=160), :] = wave[8 * block : 8 * block + 8]

    send(dot_t(w_ref[0:128, :], arranged(0)), 0, 16)
    send(dot_t(w_ref[128:256, :], arranged(8)), 8, 16)
    both = dot_t(w_ref[256:512, :], arranged(4))
    send(both[:128], 4, 16)
    send(both[128:] * sign, 12, 16)
    for e, k in enumerate(DOUBLES):
        both = dot_t(w_ref[512 + 128 * e : 640 + 128 * e, :], arranged(k))
        send(both[:64], k, 8)
        send(both[64:] * sign[:64], 16 - k, 8)


def modes_kernel(in_ref, y_ref, tr_ref, ti_ref, last_ref, out_ref):
    tr, ti = tr_ref[...], ti_ref[...]
    turned = jnp.concatenate([in_ref[pl.ds(slot, 256, stride=5), :].T for slot in range(5)], axis=0)
    high, low = split(turned)
    both = dot(jnp.concatenate([high, high, low], axis=1), y_ref[...])

    def write(modes, side, column):
        sr, si, pr, pi = modes[:32], modes[32:64], modes[64:96], modes[96:]
        square = sr * sr + si * si
        some = square > 1e-30
        scale = lax.rsqrt(jnp.maximum(square, 1e-30))
        results = (
            square * scale,
            jnp.where(some, (sr * pr + si * pi) * scale, jnp.sqrt(pr * pr + pi * pi)),
            jnp.where(some, (si * pr - sr * pi) * scale, 0.0),
        )
        for o, result in enumerate(results):
            for p in range(2):
                for half in range(2):
                    block = result[16 * p : 16 * p + 16, 128 * half : 128 * half + 128]
                    out_ref[pl.ds(16 * 48 * side + place(o, p, half, column), 16, stride=48), :] = block

    for slot in range(5):
        cos, sin = both[128 * slot : 128 * slot + 128, :256], both[128 * slot : 128 * slot + 128, 256:]
        high, low = split(jnp.concatenate([cos * tr + sin * ti, sin * tr - cos * ti], axis=0))
        data = jnp.concatenate([high, high, low], axis=0)
        if slot < 3:
            modes = dot(last_ref[...], data)
            write(modes[:128], 0, slot)
            write(modes[128:], 1, slot)
        else:
            write(dot(last_ref[:128, :], data), slot - 3, 3)


def place(o, p, half, column):
    return 16 * o + 8 * p + 4 * half + column


def spectra_kernel(in_ref, order_ref, out_ref, held, sems):
    factor = 64.0 / (4096 * 2048)
    row = lax.broadcasted_iota(jnp.int32, (128, 128), 0)
    col = lax.broadcasted_iota(jnp.int32, (128, 128), 1)
    gz = lax.axis_index("gz")
    drop = row + col + lax.axis_index("gy") + gz == 0
    order = order_ref[jnp.where(gz > 7, 1, 0)]
    copies = []
    for p in range(2):
        for half in range(2):
            at = 2 * p + half
            turned = [
                jnp.concatenate(
                    [in_ref[pl.ds(place(o, p, half, column), 32, stride=48), :] for column in range(4)], axis=0
                ).T
                for o in range(3)
            ]
            high, low = split(jnp.concatenate(turned, axis=0))
            sorted_values = dot(jnp.concatenate([high, low], axis=1), order)
            size, re, im = sorted_values[:128], sorted_values[128:256], sorted_values[256:]
            scaled = size * factor
            results = (size * scaled, (re * re + im * im) * factor, scaled * re, scaled * im)
            for o, result in enumerate(results):
                held[at, o] = jnp.where(drop, 0.0, result) if half == 0 else result
            copies.append(pltpu.make_async_copy(held.at[at], out_ref.at[:, p, pl.ds(128 * half, 128), :], sems.at[at]))
            copies[-1].start()
    for copy in copies:
        copy.wait()


def shape(*sizes):
    return jax.ShapeDtypeStruct(sizes, jnp.float32)


def shards(labels, porosity):
    count = lax.axis_size("gy")
    following = lax.ppermute(labels[:, :4, :], "gy", [((i + 1) % count, i) for i in range(count)])
    planes, ends, table = pl.pallas_call(
        planes_kernel,
        out_shape=(shape(16 * CHUNK, 128), shape(4, 24, 128), shape(8, 128)),
        in_specs=[HBM, HBM],
        out_specs=(VMEM, VMEM, VMEM),
        scratch_shapes=[
            pltpu.VMEM((6, 256, 128), jnp.int32),
            pltpu.SMEM((6,), jnp.float32),
            pltpu.VMEM((4, 256, 128), jnp.float32),
            pltpu.SemaphoreType.DMA((BLOCKS + 1,)),
        ],
        compiler_params=PARAMS,
        cost_estimate=pl.CostEstimate(flops=10_000_000, bytes_accessed=4_000_000, transcendentals=0),
        name="planes",
    )(*[pltpu.with_memory_space_constraint(array, pltpu.HBM) for array in (porosity, labels)])
    rows = pl.pallas_call(
        rows_kernel,
        out_shape=shape(16 * CHUNK, 128),
        in_specs=[VMEM, VMEM, VMEM, VMEM],
        out_specs=VMEM,
        scratch_shapes=[pltpu.VMEM((4, 32, 128), jnp.float32)],
        compiler_params=PARAMS,
        name="rows",
    )(planes, ends, table, following)
    rows = lax.all_to_all(rows.reshape(4 * CHUNK, 4, 128), "gz", 0, 0, tiled=True).reshape(16 * CHUNK, 128)
    columns = pl.pallas_call(
        columns_kernel,
        out_shape=shape(256 * 5, 128),
        in_specs=[VMEM, VMEM],
        out_specs=VMEM,
        scratch_shapes=[pltpu.VMEM((16, 32, 128), jnp.float32), pltpu.VMEM((16, 64, 128), jnp.float32)],
        compiler_params=PARAMS,
        name="columns",
    )(rows, jnp.asarray(z_matrices()))
    columns = lax.all_to_all(columns.reshape(256 * 5, 1, 128), ("gy", "gz"), 0, 0, tiled=True)
    cos, sin = twiddles()
    modes = pl.pallas_call(
        modes_kernel,
        out_shape=shape(32 * 48, 128),
        in_specs=[VMEM] * 5,
        out_specs=VMEM,
        compiler_params=PARAMS,
        name="modes",
    )(columns.reshape(256 * 5, 128), jnp.asarray(y_matrix()), jnp.asarray(cos), jnp.asarray(sin), jnp.asarray(last_matrix()))
    groups = [[16 * gy + gz for gz in (g, 15 - g) for gy in range(16)] for g in range(8)]
    modes = lax.all_to_all(modes.reshape(32, 48, 128), ("gy", "gz"), 0, 0, tiled=True, axis_index_groups=groups)
    return pl.pallas_call(
        spectra_kernel,
        out_shape=shape(4, 2, 256, 128),
        in_specs=[VMEM, VMEM],
        out_specs=HBM,
        scratch_shapes=[pltpu.VMEM((4, 4, 128, 128), jnp.float32), pltpu.SemaphoreType.DMA((4,))],
        compiler_params=PARAMS,
        name="spectra",
    )(modes.reshape(32 * 48, 128), jnp.asarray(order_matrices()))


def solution(mesh):
    placed = (P(None, "gy", "gz"), P())
    return jax.shard_map(
        shards, mesh=mesh, in_specs=placed, out_specs=P(None, None, "gy", "gz"), check_vma=False
    )
```

```python
import functools
import math

import jax
import jax.numpy as jnp
import ml_dtypes
import numpy as np
from jax import lax
from jax.experimental import pallas as pl
from jax.experimental.pallas import tpu as pltpu
from jax.sharding import PartitionSpec as P

VMEM = pl.BlockSpec(memory_space=pltpu.VMEM)
HBM = pl.BlockSpec(memory_space=pltpu.HBM)
PARAMS = pltpu.CompilerParams(vmem_limit_bytes=48 * 1024 * 1024)


def halves(matrix):
    high = matrix.astype(ml_dtypes.bfloat16)
    low = (matrix - high.astype(np.float64)).astype(ml_dtypes.bfloat16)
    return high, low


def split(value):
    high = value.astype(jnp.bfloat16)
    low = (value - high.astype(jnp.float32)).astype(jnp.bfloat16)
    return high, low


def dot(a, b):
    return lax.dot_general(a, b, (((1,), (0,)), ((), ())), preferred_element_type=jnp.float32)


def dot_t(a, b):
    return lax.dot_general(a, b, (((1,), (1,)), ((), ())), preferred_element_type=jnp.float32)


def joined(matrix, axis):
    high, low = halves(matrix)
    return np.concatenate([high, low, high], axis=axis)


def z_matrices():
    q = np.arange(128)[:, None]
    j = np.arange(128)[None, :]
    angles = [2.0 * math.pi / 2048 * ((j * (16 * q + s)) % 2048) for s in range(9)]
    return np.stack([joined(np.concatenate([np.cos(t), np.sin(t)], axis=1), 1) for t in angles])


def y_matrix():
    i = np.arange(128)[:, None]
    blocks = []
    for odd in range(2):
        m = 2 * np.arange(128)[None, :] + odd
        theta = 2.0 * math.pi / 256 * ((i * m) % 256)
        blocks.append(joined(np.concatenate([np.cos(theta), np.sin(theta)], axis=1), 0))
    return np.concatenate(blocks, axis=0)


def twiddles():
    r = np.arange(128)[:, None] % 16
    m = np.concatenate([np.arange(0, 256, 2), np.arange(1, 256, 2)])[None, :]
    phi = 2.0 * math.pi / 4096 * (m * r)
    return np.cos(phi).astype(np.float32), (-np.sin(phi)).astype(np.float32)


def last_matrix():
    w = np.zeros((4, 2, 16, 2, 2, 2, 2, 16))
    g = np.arange(16)[:, None]
    r = np.arange(16)[None, :]
    psi = 2.0 * math.pi / 16 * ((g * r) % 16)
    cos, sin = np.cos(psi), np.sin(psi)
    for field in range(2):
        for plane in range(2):
            w[2 * field, plane, :, 0, 0, field, plane] = cos
            w[2 * field, plane, :, 1, 1, field, plane] = cos
            w[2 * field, plane, :, 0, 1, field, plane] = sin
            w[2 * field, plane, :, 1, 0, field, plane] = -sin
            w[2 * field + 1, plane, :, 0, 1, field, plane] = cos
            w[2 * field + 1, plane, :, 1, 0, field, plane] = -cos
            w[2 * field + 1, plane, :, 0, 0, field, plane] = -sin
            w[2 * field + 1, plane, :, 1, 1, field, plane] = -sin
    return joined(w.reshape(128, 256), 1)


def fill(values, ids):
    value = jnp.where(ids == 1, values[1], values[0])
    for k in range(2, 6):
        value = jnp.where(ids == k, values[k], value)
    return value


def along_x(f):
    s = [(f[k] + 6.0 * f[k + 1] + f[k + 2]) * 0.125 for k in range(4)]
    return [s[2] - s[0], s[3] - s[1], s[1], s[2]]


def along_y(ext, a, first, count):
    return (
        ext[a, first + 1 : first + 1 + count, :]
        + 6.0 * ext[a, first + 2 : first + 2 + count, :]
        + ext[a, first + 3 : first + 3 + count, :]
    ) * 0.125


CHUNK = 68
BLOCKS = 4
TALL = 256 // BLOCKS


def planes_kernel(por_ref, lab_ref, out_ref, end_ref, table_ref, held, few, ext, sems):
    copies = [pltpu.make_async_copy(por_ref, few, sems.at[BLOCKS])]
    for b in range(BLOCKS):
        rows = pl.ds(TALL * b, TALL)
        copies.append(pltpu.make_async_copy(lab_ref.at[:, rows, :], held.at[:, rows, :], sems.at[b]))
    for copy in copies:
        copy.start()
    copies[0].wait()
    values = [few[k] for k in range(6)]
    for k in range(6):
        table_ref[k : k + 1, :] = jnp.full((1, 128), values[k], jnp.float32)
    table_ref[6:8, :] = jnp.zeros((2, 128), jnp.float32)
    done = 0
    for b in range(BLOCKS):
        copies[1 + b].wait()
        rows = pl.ds(TALL * b, TALL)
        for a, value in enumerate(along_x([fill(values, held[x, rows, :]) for x in range(6)])):
            ext[a, rows, :] = value
        ready = (TALL * (b + 1) - 3) // 16
        for a in range(4):
            for d in range(done, ready):
                at = CHUNK * d + 16 * a
                out_ref[at : at + 16, :] = along_y(ext, a, 16 * d, 16)
        done = ready
    for p in range(2):
        a = 2 + p
        for d in range(15):
            at = CHUNK * d + 16 * a
            edge = CHUNK * d + 64 + 2 * p
            below = along_y(ext, a, -1, 1) if d == 0 else out_ref[at - CHUNK + 15 : at - CHUNK + 16, :]
            above = along_y(ext, a, 240, 1) if d == 14 else out_ref[at + CHUNK : at + CHUNK + 1, :]
            out_ref[edge : edge + 1, :] = below
            out_ref[edge + 1 : edge + 2, :] = above
    out_ref[15 * CHUNK :, :] = jnp.zeros((CHUNK, 128), jnp.float32)
    end_ref[...] = ext[:, 232:256, :]


def rows_kernel(in_ref, end_ref, table_ref, next_ref, out_ref, ext):
    last = 15 * CHUNK
    out_ref[:last, :] = in_ref[:last, :]
    ext[:, 0:24, :] = end_ref[...]
    values = [table_ref[k : k + 1, :] for k in range(6)]
    for a, value in enumerate(along_x([fill(values, next_ref[x]) for x in range(6)])):
        ext[a, 24:28, :] = value
        out_ref[last + 16 * a : last + 16 * a + 16, :] = along_y(ext, a, 8, 16)
    for p in range(2):
        a = 2 + p
        edge = last + 64 + 2 * p
        out_ref[edge : edge + 1, :] = along_y(ext, a, 7, 1)
        out_ref[edge + 1 : edge + 2, :] = along_y(ext, a, 24, 1)


def real_transform(x):
    n = len(x)
    if n == 2:
        return [(x[0] + x[1], None), (x[0] - x[1], None)]
    even = real_transform(x[0::2])
    odd = real_transform(x[1::2])
    out = [None] * (n // 2 + 1)
    for k in range(n // 4 + 1):
        (er, ei), (dr, di) = even[k], odd[k]
        c, s = math.cos(2.0 * math.pi * k / n), math.sin(2.0 * math.pi * k / n)
        if k == 0:
            out[0] = (er + dr, None)
            out[n // 2] = (er - dr, None)
        elif 4 * k == n:
            out[k] = (er, -dr)
        else:
            tr = c * dr if di is None else c * dr + s * di
            ti = -s * dr if di is None else c * di - s * dr
            out[k] = (er + tr, ti if ei is None else ei + ti)
            out[n // 2 - k] = (er - tr, ti if ei is None else ti - ei)
    return out


def columns_kernel(in_ref, w_ref, out_ref, ext, x_ref):
    lane = lax.broadcasted_iota(jnp.int32, (16, 16, 128), 2)

    def before(x):
        rolled = pltpu.roll(x, 1, 2)
        return jnp.where(lane == 0, jnp.concatenate([rolled[15:], rolled[:15]], axis=0), rolled)

    def after(x):
        rolled = pltpu.roll(x, 127, 2)
        return jnp.where(lane == 127, jnp.concatenate([rolled[1:], rolled[:1]], axis=0), rolled)

    def along_z(x):
        return (before(x) + 6.0 * x + after(x)) * 0.125

    def rows(first, count):
        return jnp.stack([in_ref[CHUNK * d + first : CHUNK * d + first + count, :] for d in range(16)])

    for p in range(2):
        center = rows(32 + 16 * p, 16)
        ext[:, 8:24, :] = center
        ext[:, 7:8, :] = rows(64 + 2 * p, 1)
        ext[:, 24:25, :] = rows(65 + 2 * p, 1)
        grad_x = along_z(rows(16 * p, 16))
        grad_y = along_z(ext[:, 9:25, :] - ext[:, 7:23, :])
        pore = along_z(center)
        grad_z = after(pore) - before(pore)
        surface = jnp.sqrt(grad_x * grad_x + grad_y * grad_y + grad_z * grad_z + 0.01)
        x_ref[:, 16 * p : 16 * p + 16, :] = surface
        x_ref[:, 32 + 16 * p : 48 + 16 * p, :] = pore
    parts = real_transform([x_ref[d] for d in range(16)])
    sign = jnp.where(lax.broadcasted_iota(jnp.int32, (128, 128), 1) < 64, 1.0, -1.0)

    def arranged(k):
        re, im = parts[k]
        if im is None:
            im = jnp.zeros_like(re)
        top = jnp.concatenate([re, im], axis=1)
        bottom = jnp.concatenate([im, -re], axis=1)
        high, low = split(jnp.concatenate([top, bottom], axis=0))
        return jnp.concatenate([high, high, low], axis=1)

    for k in range(9):
        wave = dot_t(w_ref[k], arranged(k))
        out_ref[k] = wave
        if 0 < k < 8:
            wave = wave * sign
            for block in range(16):
                out_ref[16 - k, 8 * block : 8 * block + 8, :] = wave[120 - 8 * block : 128 - 8 * block]


def modes_kernel(in_ref, y_ref, tr_ref, ti_ref, last_ref, out_ref):
    tr, ti = tr_ref[...], ti_ref[...]
    turned = jnp.concatenate([in_ref[pl.ds(q, 256, stride=8), :].T for q in range(8)], axis=0)
    halves_of_modes = []
    for odd in range(2):
        high, low = split(turned[:, :128] - turned[:, 128:] if odd else turned[:, :128] + turned[:, 128:])
        part = dot(jnp.concatenate([high, high, low], axis=1), y_ref[384 * odd : 384 * odd + 384, :])
        halves_of_modes.append(part)
    for q in range(8):
        parts = [part[128 * q : 128 * q + 128] for part in halves_of_modes]
        cos = jnp.concatenate([part[:, :128] for part in parts], axis=1)
        sin = jnp.concatenate([part[:, 128:] for part in parts], axis=1)
        high, low = split(jnp.concatenate([cos * tr + sin * ti, sin * tr - cos * ti], axis=0))
        modes = dot(last_ref[...], jnp.concatenate([high, high, low], axis=0))
        sr, si, pr, pi = modes[:32], modes[32:64], modes[64:96], modes[96:]
        square = sr * sr + si * si
        some = square > 1e-30
        scale = lax.rsqrt(jnp.maximum(square, 1e-30))
        results = (
            square * scale,
            jnp.where(some, (sr * pr + si * pi) * scale, jnp.sqrt(pr * pr + pi * pi)),
            jnp.where(some, (si * pr - sr * pi) * scale, 0.0),
        )
        for o, result in enumerate(results):
            for p in range(2):
                for half in range(2):
                    block = result[16 * p : 16 * p + 16, 128 * half : 128 * half + 128]
                    out_ref[pl.ds(place(o, p, half, q), 16, stride=96), :] = block


def place(o, p, half, q):
    return 32 * o + 16 * p + 8 * half + q


def spectra_kernel(in_ref, out_ref, held, sems):
    factor = 64.0 / (4096 * 2048)
    row = lax.broadcasted_iota(jnp.int32, (128, 128), 0)
    col = lax.broadcasted_iota(jnp.int32, (128, 128), 1)
    device = lax.axis_index("gy") + lax.axis_index("gz")
    drop = row + col + device == 0
    eighth = lax.broadcasted_iota(jnp.int32, (8, 128), 0) == 0

    def received(o, p, odd):
        blocks = [in_ref[pl.ds(place(o, p, odd, q), 16, stride=96), :] for q in range(8)]
        upper = [jnp.where(eighth, blocks[q][8:], blocks[7 - q][8:]) for q in range(8)]
        return jnp.concatenate([half for q in range(8) for half in (blocks[q][:8], upper[q])], axis=0)

    copies = []
    for p in range(2):
        for odd in range(2):
            size, re, im = [received(o, p, odd).T for o in range(3)]
            scaled = size * factor
            results = (size * scaled, (re * re + im * im) * factor, scaled * re, scaled * im)
            for o, result in enumerate(results):
                result = result if odd else jnp.where(drop, 0.0, result)
                held[pl.ds(256 * (4 * p + o) + odd, 128, stride=2), :] = result
                if odd:
                    source = held.at[pl.ds(256 * (4 * p + o), 256), :]
                    copies.append(pltpu.make_async_copy(source, out_ref.at[o, p], sems.at[4 * p + o]))
                    copies[-1].start()
    for copy in copies:
        copy.wait()


def shape(*sizes):
    return jax.ShapeDtypeStruct(sizes, jnp.float32)


def shards(labels, porosity):
    count = lax.axis_size("gy")
    following = lax.ppermute(labels[:, :4, :], "gy", [((i + 1) % count, i) for i in range(count)])
    planes, ends, table = pl.pallas_call(
        planes_kernel,
        out_shape=(shape(16 * CHUNK, 128), shape(4, 24, 128), shape(8, 128)),
        in_specs=[HBM, HBM],
        out_specs=(VMEM, VMEM, VMEM),
        scratch_shapes=[
            pltpu.VMEM((6, 256, 128), jnp.int32),
            pltpu.SMEM((6,), jnp.float32),
            pltpu.VMEM((4, 256, 128), jnp.float32),
            pltpu.SemaphoreType.DMA((BLOCKS + 1,)),
        ],
        compiler_params=PARAMS,
        cost_estimate=pl.CostEstimate(flops=10_000_000, bytes_accessed=4_000_000, transcendentals=0),
        name="planes",
    )(*[pltpu.with_memory_space_constraint(array, pltpu.HBM) for array in (porosity, labels)])
    rows = pl.pallas_call(
        rows_kernel,
        out_shape=shape(16 * CHUNK, 128),
        in_specs=[VMEM, VMEM, VMEM, VMEM],
        out_specs=VMEM,
        scratch_shapes=[pltpu.VMEM((4, 32, 128), jnp.float32)],
        compiler_params=PARAMS,
        name="rows",
    )(planes, ends, table, following)
    rows = lax.all_to_all(rows.reshape(4 * CHUNK, 4, 128), "gz", 0, 0, tiled=True).reshape(16 * CHUNK, 128)
    columns = pl.pallas_call(
        columns_kernel,
        out_shape=shape(16, 128, 128),
        in_specs=[VMEM, VMEM],
        out_specs=VMEM,
        scratch_shapes=[pltpu.VMEM((16, 32, 128), jnp.float32), pltpu.VMEM((16, 64, 128), jnp.float32)],
        compiler_params=PARAMS,
        name="columns",
    )(rows, jnp.asarray(z_matrices()))
    columns = lax.all_to_all(columns.reshape(256, 8, 128), ("gy", "gz"), 0, 0, tiled=True)
    cos, sin = twiddles()
    modes = pl.pallas_call(
        modes_kernel,
        out_shape=shape(16 * 96, 128),
        in_specs=[VMEM] * 5,
        out_specs=VMEM,
        compiler_params=PARAMS,
        name="modes",
    )(columns.reshape(2048, 128), jnp.asarray(y_matrix()), jnp.asarray(cos), jnp.asarray(sin), jnp.asarray(last_matrix()))
    modes = lax.all_to_all(modes.reshape(16, 96, 128), "gy", 0, 0, tiled=True)
    return pl.pallas_call(
        spectra_kernel,
        out_shape=shape(4, 2, 256, 128),
        in_specs=[VMEM],
        out_specs=HBM,
        scratch_shapes=[pltpu.VMEM((8 * 256, 128), jnp.float32), pltpu.SemaphoreType.DMA((8,))],
        compiler_params=PARAMS,
        name="spectra",
    )(modes.reshape(16 * 96, 128))


def solution(mesh):
    placed = (P(None, "gy", "gz"), P())
    return jax.shard_map(
        shards, mesh=mesh, in_specs=placed, out_specs=P(None, None, "gy", "gz"), check_vma=False
    )
```

```python
import functools
import math

import jax
import jax.numpy as jnp
import ml_dtypes
import numpy as np
from jax import lax
from jax.experimental import pallas as pl
from jax.experimental.pallas import tpu as pltpu
from jax.sharding import PartitionSpec as P

VMEM = pl.BlockSpec(memory_space=pltpu.VMEM)
HBM = pl.BlockSpec(memory_space=pltpu.HBM)
PARAMS = pltpu.CompilerParams(vmem_limit_bytes=48 * 1024 * 1024)


def halves(matrix):
    high = matrix.astype(ml_dtypes.bfloat16)
    low = (matrix - high.astype(np.float64)).astype(ml_dtypes.bfloat16)
    return high, low


def split(value):
    high = value.astype(jnp.bfloat16)
    low = (value - high.astype(jnp.float32)).astype(jnp.bfloat16)
    return high, low


def dot(a, b):
    return lax.dot_general(a, b, (((1,), (0,)), ((), ())), preferred_element_type=jnp.float32)


def dot_t(a, b):
    return lax.dot_general(a, b, (((1,), (1,)), ((), ())), preferred_element_type=jnp.float32)


def joined(matrix, axis):
    high, low = halves(matrix)
    return np.concatenate([high, low, high], axis=axis)


def z_matrices():
    q = np.arange(128)[:, None]
    j = np.arange(128)[None, :]
    angles = [2.0 * math.pi / 2048 * ((j * (16 * q + s)) % 2048) for s in range(9)]
    return np.stack([joined(np.concatenate([np.cos(t), np.sin(t)], axis=1), 1) for t in angles])


def y_matrix():
    i = np.arange(128)[:, None]
    blocks = []
    for odd in range(2):
        m = 2 * np.arange(128)[None, :] + odd
        theta = 2.0 * math.pi / 256 * ((i * m) % 256)
        blocks.append(joined(np.concatenate([np.cos(theta), np.sin(theta)], axis=1), 0))
    return np.concatenate(blocks, axis=0)


def twiddles():
    r = np.arange(128)[:, None] % 16
    m = np.concatenate([np.arange(0, 256, 2), np.arange(1, 256, 2)])[None, :]
    phi = 2.0 * math.pi / 4096 * (m * r)
    return np.cos(phi).astype(np.float32), (-np.sin(phi)).astype(np.float32)


def last_matrix():
    w = np.zeros((4, 2, 16, 2, 2, 2, 2, 16))
    g = np.arange(16)[:, None]
    r = np.arange(16)[None, :]
    psi = 2.0 * math.pi / 16 * ((g * r) % 16)
    cos, sin = np.cos(psi), np.sin(psi)
    for field in range(2):
        for plane in range(2):
            w[2 * field, plane, :, 0, 0, field, plane] = cos
            w[2 * field, plane, :, 1, 1, field, plane] = cos
            w[2 * field, plane, :, 0, 1, field, plane] = sin
            w[2 * field, plane, :, 1, 0, field, plane] = -sin
            w[2 * field + 1, plane, :, 0, 1, field, plane] = cos
            w[2 * field + 1, plane, :, 1, 0, field, plane] = -cos
            w[2 * field + 1, plane, :, 0, 0, field, plane] = -sin
            w[2 * field + 1, plane, :, 1, 1, field, plane] = -sin
    return joined(w.reshape(128, 256), 1)


def fill(values, ids):
    value = jnp.where(ids == 1, values[1], values[0])
    for k in range(2, 6):
        value = jnp.where(ids == k, values[k], value)
    return value


def along_x(f):
    s = [(f[k] + 6.0 * f[k + 1] + f[k + 2]) * 0.125 for k in range(4)]
    return [s[2] - s[0], s[3] - s[1], s[1], s[2]]


def along_y(ext, a, first, count):
    return (
        ext[a, first + 1 : first + 1 + count, :]
        + 6.0 * ext[a, first + 2 : first + 2 + count, :]
        + ext[a, first + 3 : first + 3 + count, :]
    ) * 0.125


CHUNK = 68
BLOCKS = 4
TALL = 256 // BLOCKS


def planes_kernel(por_ref, lab_ref, out_ref, end_ref, table_ref, held, few, ext, sems):
    copies = [pltpu.make_async_copy(por_ref, few, sems.at[BLOCKS])]
    for b in range(BLOCKS):
        rows = pl.ds(TALL * b, TALL)
        copies.append(pltpu.make_async_copy(lab_ref.at[:, rows, :], held.at[:, rows, :], sems.at[b]))
    for copy in copies:
        copy.start()
    copies[0].wait()
    values = [few[k] for k in range(6)]
    for k in range(6):
        table_ref[k : k + 1, :] = jnp.full((1, 128), values[k], jnp.float32)
    table_ref[6:8, :] = jnp.zeros((2, 128), jnp.float32)
    done = 1
    for b in range(BLOCKS):
        copies[1 + b].wait()
        rows = pl.ds(TALL * b, TALL)
        for a, value in enumerate(along_x([fill(values, held[x, rows, :]) for x in range(6)])):
            ext[a, rows, :] = value
        ready = TALL * (b + 1) // 16
        for a in range(4):
            for d in range(done, ready):
                at = CHUNK * d + 16 * a
                out_ref[at : at + 16, :] = along_y(ext, a, 16 * d - 4, 16)
        done = ready
    for p in range(2):
        a = 2 + p
        for d in range(1, 16):
            at = CHUNK * d + 16 * a
            edge = CHUNK * d + 64 + 2 * p
            below = along_y(ext, a, 11, 1) if d == 1 else out_ref[at - CHUNK + 15 : at - CHUNK + 16, :]
            above = along_y(ext, a, 252, 1) if d == 15 else out_ref[at + CHUNK : at + CHUNK + 1, :]
            out_ref[edge : edge + 1, :] = below
            out_ref[edge + 1 : edge + 2, :] = above
    out_ref[:CHUNK, :] = jnp.zeros((CHUNK, 128), jnp.float32)
    end_ref[...] = ext[:, 0:24, :]


def rows_kernel(in_ref, end_ref, table_ref, before_ref, out_ref, ext):
    out_ref[CHUNK:, :] = in_ref[CHUNK:, :]
    ext[:, 8:32, :] = end_ref[...]
    values = [table_ref[k : k + 1, :] for k in range(6)]
    for a, value in enumerate(along_x([fill(values, before_ref[x]) for x in range(6)])):
        ext[a, 4:8, :] = value
        out_ref[16 * a : 16 * a + 16, :] = along_y(ext, a, 4, 16)
    for p in range(2):
        edge = 64 + 2 * p
        out_ref[edge : edge + 1, :] = along_y(ext, 2 + p, 3, 1)
        out_ref[edge + 1 : edge + 2, :] = along_y(ext, 2 + p, 20, 1)


def real_transform(x):
    n = len(x)
    if n == 2:
        return [(x[0] + x[1], None), (x[0] - x[1], None)]
    even = real_transform(x[0::2])
    odd = real_transform(x[1::2])
    out = [None] * (n // 2 + 1)
    for k in range(n // 4 + 1):
        (er, ei), (dr, di) = even[k], odd[k]
        c, s = math.cos(2.0 * math.pi * k / n), math.sin(2.0 * math.pi * k / n)
        if k == 0:
            out[0] = (er + dr, None)
            out[n // 2] = (er - dr, None)
        elif 4 * k == n:
            out[k] = (er, -dr)
        else:
            tr = c * dr if di is None else c * dr + s * di
            ti = -s * dr if di is None else c * di - s * dr
            out[k] = (er + tr, ti if ei is None else ei + ti)
            out[n // 2 - k] = (er - tr, ti if ei is None else ti - ei)
    return out


def columns_kernel(in_ref, w_ref, out_ref, ext, x_ref):
    lane = lax.broadcasted_iota(jnp.int32, (16, 16, 128), 2)

    def before(x):
        rolled = pltpu.roll(x, 1, 2)
        return jnp.where(lane == 0, jnp.concatenate([rolled[15:], rolled[:15]], axis=0), rolled)

    def after(x):
        rolled = pltpu.roll(x, 127, 2)
        return jnp.where(lane == 127, jnp.concatenate([rolled[1:], rolled[:1]], axis=0), rolled)

    def along_z(x):
        return (before(x) + 6.0 * x + after(x)) * 0.125

    def rows(first, count):
        return jnp.stack([in_ref[CHUNK * d + first : CHUNK * d + first + count, :] for d in range(16)])

    for p in range(2):
        center = rows(32 + 16 * p, 16)
        ext[:, 8:24, :] = center
        ext[:, 7:8, :] = rows(64 + 2 * p, 1)
        ext[:, 24:25, :] = rows(65 + 2 * p, 1)
        grad_x = along_z(rows(16 * p, 16))
        grad_y = along_z(ext[:, 9:25, :] - ext[:, 7:23, :])
        pore = along_z(center)
        grad_z = after(pore) - before(pore)
        surface = jnp.sqrt(grad_x * grad_x + grad_y * grad_y + grad_z * grad_z + 0.01)
        x_ref[:, 16 * p : 16 * p + 16, :] = surface
        x_ref[:, 32 + 16 * p : 48 + 16 * p, :] = pore
    parts = real_transform([x_ref[d] for d in range(16)])
    sign = jnp.where(lax.broadcasted_iota(jnp.int32, (128, 128), 1) < 64, 1.0, -1.0)

    def arranged(k):
        re, im = parts[k]
        if im is None:
            im = jnp.zeros_like(re)
        top = jnp.concatenate([re, im], axis=1)
        bottom = jnp.concatenate([im, -re], axis=1)
        high, low = split(jnp.concatenate([top, bottom], axis=0))
        return jnp.concatenate([high, high, low], axis=1)

    for k in range(9):
        wave = dot_t(w_ref[k], arranged(k))
        out_ref[k] = wave
        if 0 < k < 8:
            wave = wave * sign
            for block in range(16):
                out_ref[16 - k, 8 * block : 8 * block + 8, :] = wave[120 - 8 * block : 128 - 8 * block]


def modes_kernel(in_ref, y_ref, tr_ref, ti_ref, last_ref, out_ref):
    tr, ti = tr_ref[...], ti_ref[...]
    turned = jnp.concatenate([in_ref[pl.ds(q, 256, stride=8), :].T for q in range(8)], axis=0)
    halves_of_modes = []
    for odd in range(2):
        high, low = split(turned[:, :128] - turned[:, 128:] if odd else turned[:, :128] + turned[:, 128:])
        part = dot(jnp.concatenate([high, high, low], axis=1), y_ref[384 * odd : 384 * odd + 384, :])
        halves_of_modes.append(part)
    for q in range(8):
        parts = [part[128 * q : 128 * q + 128] for part in halves_of_modes]
        cos = jnp.concatenate([part[:, :128] for part in parts], axis=1)
        sin = jnp.concatenate([part[:, 128:] for part in parts], axis=1)
        high, low = split(jnp.concatenate([cos * tr + sin * ti, sin * tr - cos * ti], axis=0))
        modes = dot(last_ref[...], jnp.concatenate([high, high, low], axis=0))
        sr, si, pr, pi = modes[:32], modes[32:64], modes[64:96], modes[96:]
        square = sr * sr + si * si
        some = square > 1e-30
        scale = lax.rsqrt(jnp.maximum(square, 1e-30))
        results = (
            square * scale,
            jnp.where(some, (sr * pr + si * pi) * scale, jnp.sqrt(pr * pr + pi * pi)),
            jnp.where(some, (si * pr - sr * pi) * scale, 0.0),
        )
        for o, result in enumerate(results):
            for p in range(2):
                for half in range(2):
                    block = result[16 * p : 16 * p + 16, 128 * half : 128 * half + 128]
                    out_ref[pl.ds(place(o, p, half, q), 16, stride=96), :] = block


def place(o, p, half, q):
    return 32 * o + 16 * p + 8 * half + q


def spectra_kernel(in_ref, out_ref, held, sems):
    factor = 64.0 / (4096 * 2048)
    row = lax.broadcasted_iota(jnp.int32, (128, 128), 0)
    col = lax.broadcasted_iota(jnp.int32, (128, 128), 1)
    device = lax.axis_index("gy") + lax.axis_index("gz")
    drop = row + col + device == 0
    eighth = lax.broadcasted_iota(jnp.int32, (8, 128), 0) == 0

    def received(o, p, odd):
        blocks = [in_ref[pl.ds(place(o, p, odd, q), 16, stride=96), :] for q in range(8)]
        upper = [jnp.where(eighth, blocks[q][8:], blocks[7 - q][8:]) for q in range(8)]
        return jnp.concatenate([half for q in range(8) for half in (blocks[q][:8], upper[q])], axis=0)

    copies = []
    for p in range(2):
        for odd in range(2):
            size, re, im = [received(o, p, odd).T for o in range(3)]
            scaled = size * factor
            results = (size * scaled, (re * re + im * im) * factor, scaled * re, scaled * im)
            for o, result in enumerate(results):
                result = result if odd else jnp.where(drop, 0.0, result)
                held[pl.ds(256 * (4 * p + o) + odd, 128, stride=2), :] = result
                if odd:
                    source = held.at[pl.ds(256 * (4 * p + o), 256), :]
                    copies.append(pltpu.make_async_copy(source, out_ref.at[o, p], sems.at[4 * p + o]))
                    copies[-1].start()
    for copy in copies:
        copy.wait()


def shape(*sizes):
    return jax.ShapeDtypeStruct(sizes, jnp.float32)


def shards(labels, porosity):
    count = lax.axis_size("gy")
    preceding = lax.ppermute(labels[:, -4:, :], "gy", [(i, (i + 1) % count) for i in range(count)])
    planes, ends, table = pl.pallas_call(
        planes_kernel,
        out_shape=(shape(16 * CHUNK, 128), shape(4, 24, 128), shape(8, 128)),
        in_specs=[HBM, HBM],
        out_specs=(VMEM, VMEM, VMEM),
        scratch_shapes=[
            pltpu.VMEM((6, 256, 128), jnp.int32),
            pltpu.SMEM((6,), jnp.float32),
            pltpu.VMEM((4, 256, 128), jnp.float32),
            pltpu.SemaphoreType.DMA((BLOCKS + 1,)),
        ],
        compiler_params=PARAMS,
        cost_estimate=pl.CostEstimate(flops=10_000_000, bytes_accessed=4_000_000, transcendentals=0),
        name="planes",
    )(*[pltpu.with_memory_space_constraint(array, pltpu.HBM) for array in (porosity, labels)])
    rows = pl.pallas_call(
        rows_kernel,
        out_shape=shape(16 * CHUNK, 128),
        in_specs=[VMEM, VMEM, VMEM, VMEM],
        out_specs=VMEM,
        scratch_shapes=[pltpu.VMEM((4, 32, 128), jnp.float32)],
        compiler_params=PARAMS,
        name="rows",
    )(planes, ends, table, preceding)
    rows = lax.all_to_all(rows.reshape(4 * CHUNK, 4, 128), "gz", 0, 0, tiled=True).reshape(16 * CHUNK, 128)
    columns = pl.pallas_call(
        columns_kernel,
        out_shape=shape(16, 128, 128),
        in_specs=[VMEM, VMEM],
        out_specs=VMEM,
        scratch_shapes=[pltpu.VMEM((16, 32, 128), jnp.float32), pltpu.VMEM((16, 64, 128), jnp.float32)],
        compiler_params=PARAMS,
        name="columns",
    )(rows, jnp.asarray(z_matrices()))
    columns = lax.all_to_all(columns.reshape(256, 8, 128), ("gy", "gz"), 0, 0, tiled=True)
    cos, sin = twiddles()
    modes = pl.pallas_call(
        modes_kernel,
        out_shape=shape(16 * 96, 128),
        in_specs=[VMEM] * 5,
        out_specs=VMEM,
        compiler_params=PARAMS,
        name="modes",
    )(columns.reshape(2048, 128), jnp.asarray(y_matrix()), jnp.asarray(cos), jnp.asarray(sin), jnp.asarray(last_matrix()))
    modes = lax.all_to_all(modes.reshape(16, 96, 128), "gy", 0, 0, tiled=True)
    return pl.pallas_call(
        spectra_kernel,
        out_shape=shape(4, 2, 256, 128),
        in_specs=[VMEM],
        out_specs=HBM,
        scratch_shapes=[pltpu.VMEM((8 * 256, 128), jnp.float32), pltpu.SemaphoreType.DMA((8,))],
        compiler_params=PARAMS,
        name="spectra",
    )(modes.reshape(16 * 96, 128))


def solution(mesh):
    placed = (P(None, "gy", "gz"), P())
    return jax.shard_map(
        shards, mesh=mesh, in_specs=placed, out_specs=P(None, None, "gy", "gz"), check_vma=False
    )
```

```python
import functools
import math

import jax
import jax.numpy as jnp
import ml_dtypes
import numpy as np
from jax import lax
from jax.experimental import pallas as pl
from jax.experimental.pallas import tpu as pltpu
from jax.sharding import PartitionSpec as P

VMEM = pl.BlockSpec(memory_space=pltpu.VMEM)
HBM = pl.BlockSpec(memory_space=pltpu.HBM)
PARAMS = pltpu.CompilerParams(vmem_limit_bytes=48 * 1024 * 1024)


def halves(matrix):
    high = matrix.astype(ml_dtypes.bfloat16)
    low = (matrix - high.astype(np.float64)).astype(ml_dtypes.bfloat16)
    return high, low


def split(value):
    high = value.astype(jnp.bfloat16)
    low = (value - high.astype(jnp.float32)).astype(jnp.bfloat16)
    return high, low


def dot(a, b):
    return lax.dot_general(a, b, (((1,), (0,)), ((), ())), preferred_element_type=jnp.float32)


def dot_t(a, b):
    return lax.dot_general(a, b, (((1,), (1,)), ((), ())), preferred_element_type=jnp.float32)


def joined(matrix, axis):
    high, low = halves(matrix)
    return np.concatenate([high, low, high], axis=axis)


def z_matrices():
    q = np.arange(128)[:, None]
    j = np.arange(128)[None, :]
    angles = [2.0 * math.pi / 2048 * ((j * (16 * q + s)) % 2048) for s in range(9)]
    return np.stack([joined(np.concatenate([np.cos(t), np.sin(t)], axis=1), 1) for t in angles])


def y_matrix():
    i = np.arange(128)[:, None]
    blocks = []
    for odd in range(2):
        m = 2 * np.arange(128)[None, :] + odd
        theta = 2.0 * math.pi / 256 * ((i * m) % 256)
        blocks.append(joined(np.concatenate([np.cos(theta), np.sin(theta)], axis=1), 0))
    return np.concatenate(blocks, axis=0)


def twiddles():
    r = np.arange(128)[:, None] % 16
    m = np.concatenate([np.arange(0, 256, 2), np.arange(1, 256, 2)])[None, :]
    phi = 2.0 * math.pi / 4096 * (m * r)
    return np.cos(phi).astype(np.float32), (-np.sin(phi)).astype(np.float32)


def last_matrix():
    w = np.zeros((4, 2, 16, 2, 2, 2, 2, 16))
    g = np.arange(16)[:, None]
    r = np.arange(16)[None, :]
    psi = 2.0 * math.pi / 16 * ((g * r) % 16)
    cos, sin = np.cos(psi), np.sin(psi)
    for field in range(2):
        for plane in range(2):
            w[2 * field, plane, :, 0, 0, field, plane] = cos
            w[2 * field, plane, :, 1, 1, field, plane] = cos
            w[2 * field, plane, :, 0, 1, field, plane] = sin
            w[2 * field, plane, :, 1, 0, field, plane] = -sin
            w[2 * field + 1, plane, :, 0, 1, field, plane] = cos
            w[2 * field + 1, plane, :, 1, 0, field, plane] = -cos
            w[2 * field + 1, plane, :, 0, 0, field, plane] = -sin
            w[2 * field + 1, plane, :, 1, 1, field, plane] = -sin
    return joined(w.reshape(128, 256), 1)


def fill(values, ids):
    value = jnp.where(ids == 1, values[1], values[0])
    for k in range(2, 6):
        value = jnp.where(ids == k, values[k], value)
    return value


def along_x(f):
    s = [(f[k] + 6.0 * f[k + 1] + f[k + 2]) * 0.125 for k in range(4)]
    return [s[2] - s[0], s[3] - s[1], s[1], s[2]]


def along_y(ext, a, first, count):
    return (
        ext[a, first + 1 : first + 1 + count, :]
        + 6.0 * ext[a, first + 2 : first + 2 + count, :]
        + ext[a, first + 3 : first + 3 + count, :]
    ) * 0.125


CHUNK = 68
BLOCKS = 4
TALL = 256 // BLOCKS


def planes_kernel(por_ref, lab_ref, out_ref, end_ref, table_ref, held, few, ext, sems):
    copies = [pltpu.make_async_copy(por_ref, few, sems.at[BLOCKS])]
    for b in range(BLOCKS):
        rows = pl.ds(TALL * b, TALL)
        copies.append(pltpu.make_async_copy(lab_ref.at[:, rows, :], held.at[:, rows, :], sems.at[b]))
    for copy in copies:
        copy.start()
    copies[0].wait()
    values = [few[k] for k in range(6)]
    for k in range(6):
        table_ref[k : k + 1, :] = jnp.full((1, 128), values[k], jnp.float32)
    table_ref[6:8, :] = jnp.zeros((2, 128), jnp.float32)
    done = 0
    for b in range(BLOCKS):
        copies[1 + b].wait()
        rows = pl.ds(TALL * b, TALL)
        for a, value in enumerate(along_x([fill(values, held[x, rows, :]) for x in range(6)])):
            ext[a, rows, :] = value
        ready = (TALL * (b + 1) - 3) // 16
        for a in range(4):
            for d in range(done, ready):
                at = CHUNK * d + 16 * a
                out_ref[at : at + 16, :] = along_y(ext, a, 16 * d, 16)
        done = ready
    for p in range(2):
        a = 2 + p
        for d in range(15):
            at = CHUNK * d + 16 * a
            edge = CHUNK * d + 64 + 2 * p
            below = along_y(ext, a, -1, 1) if d == 0 else out_ref[at - CHUNK + 15 : at - CHUNK + 16, :]
            above = along_y(ext, a, 240, 1) if d == 14 else out_ref[at + CHUNK : at + CHUNK + 1, :]
            out_ref[edge : edge + 1, :] = below
            out_ref[edge + 1 : edge + 2, :] = above
    out_ref[15 * CHUNK :, :] = jnp.zeros((CHUNK, 128), jnp.float32)
    end_ref[...] = ext[:, 232:256, :]


def rows_kernel(in_ref, end_ref, table_ref, next_ref, out_ref, ext):
    last = 15 * CHUNK
    out_ref[:last, :] = in_ref[:last, :]
    ext[:, 0:24, :] = end_ref[...]
    values = [table_ref[k : k + 1, :] for k in range(6)]
    for a, value in enumerate(along_x([fill(values, next_ref[x, 0:4, :]) for x in range(6)])):
        ext[a, 24:28, :] = value
        out_ref[last + 16 * a : last + 16 * a + 16, :] = along_y(ext, a, 8, 16)
    for p in range(2):
        a = 2 + p
        edge = last + 64 + 2 * p
        out_ref[edge : edge + 1, :] = along_y(ext, a, 7, 1)
        out_ref[edge + 1 : edge + 2, :] = along_y(ext, a, 24, 1)


def real_transform(x):
    n = len(x)
    if n == 2:
        return [(x[0] + x[1], None), (x[0] - x[1], None)]
    even = real_transform(x[0::2])
    odd = real_transform(x[1::2])
    out = [None] * (n // 2 + 1)
    for k in range(n // 4 + 1):
        (er, ei), (dr, di) = even[k], odd[k]
        c, s = math.cos(2.0 * math.pi * k / n), math.sin(2.0 * math.pi * k / n)
        if k == 0:
            out[0] = (er + dr, None)
            out[n // 2] = (er - dr, None)
        elif 4 * k == n:
            out[k] = (er, -dr)
        else:
            tr = c * dr if di is None else c * dr + s * di
            ti = -s * dr if di is None else c * di - s * dr
            out[k] = (er + tr, ti if ei is None else ei + ti)
            out[n // 2 - k] = (er - tr, ti if ei is None else ti - ei)
    return out


def columns_kernel(in_ref, w_ref, out_ref, ext, x_ref):
    lane = lax.broadcasted_iota(jnp.int32, (16, 16, 128), 2)

    def before(x):
        rolled = pltpu.roll(x, 1, 2)
        return jnp.where(lane == 0, jnp.concatenate([rolled[15:], rolled[:15]], axis=0), rolled)

    def after(x):
        rolled = pltpu.roll(x, 127, 2)
        return jnp.where(lane == 127, jnp.concatenate([rolled[1:], rolled[:1]], axis=0), rolled)

    def along_z(x):
        return (before(x) + 6.0 * x + after(x)) * 0.125

    def rows(first, count):
        return jnp.stack([in_ref[CHUNK * d + first : CHUNK * d + first + count, :] for d in range(16)])

    for p in range(2):
        center = rows(32 + 16 * p, 16)
        ext[:, 8:24, :] = center
        ext[:, 7:8, :] = rows(64 + 2 * p, 1)
        ext[:, 24:25, :] = rows(65 + 2 * p, 1)
        grad_x = along_z(rows(16 * p, 16))
        grad_y = along_z(ext[:, 9:25, :] - ext[:, 7:23, :])
        pore = along_z(center)
        grad_z = after(pore) - before(pore)
        surface = jnp.sqrt(grad_x * grad_x + grad_y * grad_y + grad_z * grad_z + 0.01)
        x_ref[:, 16 * p : 16 * p + 16, :] = surface
        x_ref[:, 32 + 16 * p : 48 + 16 * p, :] = pore
    parts = real_transform([x_ref[d] for d in range(16)])
    sign = jnp.where(lax.broadcasted_iota(jnp.int32, (128, 128), 1) < 64, 1.0, -1.0)

    def arranged(k):
        re, im = parts[k]
        if im is None:
            im = jnp.zeros_like(re)
        top = jnp.concatenate([re, im], axis=1)
        bottom = jnp.concatenate([im, -re], axis=1)
        high, low = split(jnp.concatenate([top, bottom], axis=0))
        return jnp.concatenate([high, high, low], axis=1)

    for k in range(9):
        wave = dot_t(w_ref[k], arranged(k))
        out_ref[k] = wave
        if 0 < k < 8:
            wave = wave * sign
            for block in range(16):
                out_ref[16 - k, 8 * block : 8 * block + 8, :] = wave[120 - 8 * block : 128 - 8 * block]


def modes_kernel(in_ref, y_ref, tr_ref, ti_ref, last_ref, out_ref):
    tr, ti = tr_ref[...], ti_ref[...]
    turned = jnp.concatenate([in_ref[pl.ds(q, 256, stride=8), :].T for q in range(8)], axis=0)
    halves_of_modes = []
    for odd in range(2):
        high, low = split(turned[:, :128] - turned[:, 128:] if odd else turned[:, :128] + turned[:, 128:])
        part = dot(jnp.concatenate([high, high, low], axis=1), y_ref[384 * odd : 384 * odd + 384, :])
        halves_of_modes.append(part)
    for q in range(8):
        parts = [part[128 * q : 128 * q + 128] for part in halves_of_modes]
        cos = jnp.concatenate([part[:, :128] for part in parts], axis=1)
        sin = jnp.concatenate([part[:, 128:] for part in parts], axis=1)
        high, low = split(jnp.concatenate([cos * tr + sin * ti, sin * tr - cos * ti], axis=0))
        modes = dot(last_ref[...], jnp.concatenate([high, high, low], axis=0))
        sr, si, pr, pi = modes[:32], modes[32:64], modes[64:96], modes[96:]
        square = sr * sr + si * si
        some = square > 1e-30
        scale = lax.rsqrt(jnp.maximum(square, 1e-30))
        results = (
            square * scale,
            jnp.where(some, (sr * pr + si * pi) * scale, jnp.sqrt(pr * pr + pi * pi)),
            jnp.where(some, (si * pr - sr * pi) * scale, 0.0),
        )
        for o, result in enumerate(results):
            for p in range(2):
                for half in range(2):
                    block = result[16 * p : 16 * p + 16, 128 * half : 128 * half + 128]
                    out_ref[pl.ds(place(o, p, half, q), 16, stride=96), :] = block


def place(o, p, half, q):
    return 32 * o + 16 * p + 8 * half + q


def spectra_kernel(in_ref, out_ref, held, sems):
    factor = 64.0 / (4096 * 2048)
    row = lax.broadcasted_iota(jnp.int32, (128, 128), 0)
    col = lax.broadcasted_iota(jnp.int32, (128, 128), 1)
    device = lax.axis_index("gy") + lax.axis_index("gz")
    drop = row + col + device == 0
    eighth = lax.broadcasted_iota(jnp.int32, (8, 128), 0) == 0

    def received(o, p, odd):
        blocks = [in_ref[pl.ds(place(o, p, odd, q), 16, stride=96), :] for q in range(8)]
        upper = [jnp.where(eighth, blocks[q][8:], blocks[7 - q][8:]) for q in range(8)]
        return jnp.concatenate([half for q in range(8) for half in (blocks[q][:8], upper[q])], axis=0)

    copies = []
    for p in range(2):
        for odd in range(2):
            size, re, im = [received(o, p, odd).T for o in range(3)]
            scaled = size * factor
            results = (size * scaled, (re * re + im * im) * factor, scaled * re, scaled * im)
            for o, result in enumerate(results):
                result = result if odd else jnp.where(drop, 0.0, result)
                held[pl.ds(256 * (4 * p + o) + odd, 128, stride=2), :] = result
                if odd:
                    source = held.at[pl.ds(256 * (4 * p + o), 256), :]
                    copies.append(pltpu.make_async_copy(source, out_ref.at[o, p], sems.at[4 * p + o]))
                    copies[-1].start()
    for copy in copies:
        copy.wait()


def shape(*sizes):
    return jax.ShapeDtypeStruct(sizes, jnp.float32)


def shards(labels, porosity):
    count = lax.axis_size("gy")
    following = lax.ppermute(labels[:, :8, :], "gy", [((i + 1) % count, i) for i in range(count)])
    planes, ends, table = pl.pallas_call(
        planes_kernel,
        out_shape=(shape(16 * CHUNK, 128), shape(4, 24, 128), shape(8, 128)),
        in_specs=[HBM, HBM],
        out_specs=(VMEM, VMEM, VMEM),
        scratch_shapes=[
            pltpu.VMEM((6, 256, 128), jnp.int32),
            pltpu.SMEM((6,), jnp.float32),
            pltpu.VMEM((4, 256, 128), jnp.float32),
            pltpu.SemaphoreType.DMA((BLOCKS + 1,)),
        ],
        compiler_params=PARAMS,
        cost_estimate=pl.CostEstimate(flops=10_000_000, bytes_accessed=4_000_000, transcendentals=0),
        name="planes",
    )(*[pltpu.with_memory_space_constraint(array, pltpu.HBM) for array in (porosity, labels)])
    rows = pl.pallas_call(
        rows_kernel,
        out_shape=shape(16 * CHUNK, 128),
        in_specs=[VMEM, VMEM, VMEM, VMEM],
        out_specs=VMEM,
        scratch_shapes=[pltpu.VMEM((4, 32, 128), jnp.float32)],
        compiler_params=PARAMS,
        name="rows",
    )(planes, ends, table, following)
    rows = lax.all_to_all(rows.reshape(4 * CHUNK, 4, 128), "gz", 0, 0, tiled=True).reshape(16 * CHUNK, 128)
    columns = pl.pallas_call(
        columns_kernel,
        out_shape=shape(16, 128, 128),
        in_specs=[VMEM, VMEM],
        out_specs=VMEM,
        scratch_shapes=[pltpu.VMEM((16, 32, 128), jnp.float32), pltpu.VMEM((16, 64, 128), jnp.float32)],
        compiler_params=PARAMS,
        name="columns",
    )(rows, jnp.asarray(z_matrices()))
    columns = lax.all_to_all(columns.reshape(256, 8, 128), ("gy", "gz"), 0, 0, tiled=True)
    cos, sin = twiddles()
    modes = pl.pallas_call(
        modes_kernel,
        out_shape=shape(16 * 96, 128),
        in_specs=[VMEM] * 5,
        out_specs=VMEM,
        compiler_params=PARAMS,
        name="modes",
    )(columns.reshape(2048, 128), jnp.asarray(y_matrix()), jnp.asarray(cos), jnp.asarray(sin), jnp.asarray(last_matrix()))
    modes = lax.all_to_all(modes.reshape(16, 96, 128), "gy", 0, 0, tiled=True)
    return pl.pallas_call(
        spectra_kernel,
        out_shape=shape(4, 2, 256, 128),
        in_specs=[VMEM],
        out_specs=HBM,
        scratch_shapes=[pltpu.VMEM((8 * 256, 128), jnp.float32), pltpu.SemaphoreType.DMA((8,))],
        compiler_params=PARAMS,
        name="spectra",
    )(modes.reshape(16 * 96, 128))


def solution(mesh):
    placed = (P(None, "gy", "gz"), P())
    return jax.shard_map(
        shards, mesh=mesh, in_specs=placed, out_specs=P(None, None, "gy", "gz"), check_vma=False
    )
```

```python
import functools
import math

import jax
import jax.numpy as jnp
import ml_dtypes
import numpy as np
from jax import lax
from jax.experimental import pallas as pl
from jax.experimental.pallas import tpu as pltpu
from jax.sharding import PartitionSpec as P

VMEM = pl.BlockSpec(memory_space=pltpu.VMEM)
HBM = pl.BlockSpec(memory_space=pltpu.HBM)
PARAMS = pltpu.CompilerParams(vmem_limit_bytes=48 * 1024 * 1024)


def halves(matrix):
    high = matrix.astype(ml_dtypes.bfloat16)
    low = (matrix - high.astype(np.float64)).astype(ml_dtypes.bfloat16)
    return high, low


def split(value):
    high = value.astype(jnp.bfloat16)
    low = (value - high.astype(jnp.float32)).astype(jnp.bfloat16)
    return high, low


def dot(a, b):
    return lax.dot_general(a, b, (((1,), (0,)), ((), ())), preferred_element_type=jnp.float32)


def dot_t(a, b):
    return lax.dot_general(a, b, (((1,), (1,)), ((), ())), preferred_element_type=jnp.float32)


def joined(matrix, axis):
    high, low = halves(matrix)
    return np.concatenate([high, low, high], axis=axis)


def z_matrices():
    q = np.arange(128)[:, None]
    j = np.arange(128)[None, :]
    angles = [2.0 * math.pi / 2048 * ((j * (16 * q + s)) % 2048) for s in range(9)]
    return np.stack([joined(np.concatenate([np.cos(t), np.sin(t)], axis=1), 1) for t in angles])


def y_matrix():
    i = np.arange(128)[:, None]
    blocks = []
    for odd in range(2):
        m = 2 * np.arange(128)[None, :] + odd
        theta = 2.0 * math.pi / 256 * ((i * m) % 256)
        blocks.append(joined(np.concatenate([np.cos(theta), np.sin(theta)], axis=1), 0))
    return np.concatenate(blocks, axis=0)


def twiddles():
    r = np.arange(128)[:, None] % 16
    m = np.concatenate([np.arange(0, 256, 2), np.arange(1, 256, 2)])[None, :]
    phi = 2.0 * math.pi / 4096 * (m * r)
    return np.cos(phi).astype(np.float32), (-np.sin(phi)).astype(np.float32)


def last_matrix():
    w = np.zeros((4, 2, 16, 2, 2, 2, 2, 16))
    g = np.arange(16)[:, None]
    r = np.arange(16)[None, :]
    psi = 2.0 * math.pi / 16 * ((g * r) % 16)
    cos, sin = np.cos(psi), np.sin(psi)
    for field in range(2):
        for plane in range(2):
            w[2 * field, plane, :, 0, 0, field, plane] = cos
            w[2 * field, plane, :, 1, 1, field, plane] = cos
            w[2 * field, plane, :, 0, 1, field, plane] = sin
            w[2 * field, plane, :, 1, 0, field, plane] = -sin
            w[2 * field + 1, plane, :, 0, 1, field, plane] = cos
            w[2 * field + 1, plane, :, 1, 0, field, plane] = -cos
            w[2 * field + 1, plane, :, 0, 0, field, plane] = -sin
            w[2 * field + 1, plane, :, 1, 1, field, plane] = -sin
    return joined(w.reshape(128, 256), 1)


def fill(values, ids):
    value = jnp.where(ids == 1, values[1], values[0])
    for k in range(2, 6):
        value = jnp.where(ids == k, values[k], value)
    return value


def along_x(f):
    s = [(f[k] + 6.0 * f[k + 1] + f[k + 2]) * 0.125 for k in range(4)]
    return [s[2] - s[0], s[3] - s[1], s[1], s[2]]


def along_y(ext, a, first, count):
    return (
        ext[a, first + 1 : first + 1 + count, :]
        + 6.0 * ext[a, first + 2 : first + 2 + count, :]
        + ext[a, first + 3 : first + 3 + count, :]
    ) * 0.125


CHUNK = 68
BLOCKS = 4
TALL = 256 // BLOCKS


def planes_kernel(por_ref, lab_ref, out_ref, end_ref, table_ref, held, few, ext, sems):
    copies = [pltpu.make_async_copy(por_ref, few, sems.at[BLOCKS])]
    for b in range(BLOCKS):
        rows = pl.ds(TALL * b, TALL)
        copies.append(pltpu.make_async_copy(lab_ref.at[:, rows, :], held.at[:, rows, :], sems.at[b]))
    for copy in copies:
        copy.start()
    copies[0].wait()
    values = [few[k] for k in range(6)]
    for k in range(6):
        table_ref[k : k + 1, :] = jnp.full((1, 128), values[k], jnp.float32)
    table_ref[6:8, :] = jnp.zeros((2, 128), jnp.float32)
    done = 0
    for b in range(BLOCKS):
        copies[1 + b].wait()
        rows = pl.ds(TALL * b, TALL)
        for a, value in enumerate(along_x([fill(values, held[x, rows, :]) for x in range(6)])):
            ext[a, rows, :] = value
        ready = (TALL * (b + 1) - 3) // 16
        for a in range(4):
            for d in range(done, ready):
                at = CHUNK * d + 16 * a
                out_ref[at : at + 16, :] = along_y(ext, a, 16 * d, 16)
        done = ready
    for p in range(2):
        a = 2 + p
        for d in range(15):
            at = CHUNK * d + 16 * a
            edge = CHUNK * d + 64 + 2 * p
            below = along_y(ext, a, -1, 1) if d == 0 else out_ref[at - CHUNK + 15 : at - CHUNK + 16, :]
            above = along_y(ext, a, 240, 1) if d == 14 else out_ref[at + CHUNK : at + CHUNK + 1, :]
            out_ref[edge : edge + 1, :] = below
            out_ref[edge + 1 : edge + 2, :] = above
    out_ref[15 * CHUNK :, :] = jnp.zeros((CHUNK, 128), jnp.float32)
    end_ref[...] = ext[:, 232:256, :]


def rows_kernel(in_ref, end_ref, table_ref, next_ref, out_ref, ext):
    last = 15 * CHUNK
    out_ref[:last, :] = in_ref[:last, :]
    ext[:, 0:24, :] = end_ref[...]
    values = [table_ref[k : k + 1, :] for k in range(6)]
    for a, value in enumerate(along_x([fill(values, next_ref[x]) for x in range(6)])):
        ext[a, 24:28, :] = value
        out_ref[last + 16 * a : last + 16 * a + 16, :] = along_y(ext, a, 8, 16)
    for p in range(2):
        a = 2 + p
        edge = last + 64 + 2 * p
        out_ref[edge : edge + 1, :] = along_y(ext, a, 7, 1)
        out_ref[edge + 1 : edge + 2, :] = along_y(ext, a, 24, 1)


def real_transform(x):
    n = len(x)
    if n == 2:
        return [(x[0] + x[1], None), (x[0] - x[1], None)]
    even = real_transform(x[0::2])
    odd = real_transform(x[1::2])
    out = [None] * (n // 2 + 1)
    for k in range(n // 4 + 1):
        (er, ei), (dr, di) = even[k], odd[k]
        c, s = math.cos(2.0 * math.pi * k / n), math.sin(2.0 * math.pi * k / n)
        if k == 0:
            out[0] = (er + dr, None)
            out[n // 2] = (er - dr, None)
        elif 4 * k == n:
            out[k] = (er, -dr)
        else:
            tr = c * dr if di is None else c * dr + s * di
            ti = -s * dr if di is None else c * di - s * dr
            out[k] = (er + tr, ti if ei is None else ei + ti)
            out[n // 2 - k] = (er - tr, ti if ei is None else ti - ei)
    return out


def columns_kernel(in_ref, w_ref, out_ref, ext, x_ref):
    lane = lax.broadcasted_iota(jnp.int32, (16, 16, 128), 2)

    def before(x):
        rolled = pltpu.roll(x, 1, 2)
        return jnp.where(lane == 0, jnp.concatenate([rolled[15:], rolled[:15]], axis=0), rolled)

    def after(x):
        rolled = pltpu.roll(x, 127, 2)
        return jnp.where(lane == 127, jnp.concatenate([rolled[1:], rolled[:1]], axis=0), rolled)

    def along_z(x):
        return (before(x) + 6.0 * x + after(x)) * 0.125

    def rows(first, count):
        return jnp.stack([in_ref[CHUNK * d + first : CHUNK * d + first + count, :] for d in range(16)])

    for p in range(2):
        center = rows(32 + 16 * p, 16)
        ext[:, 8:24, :] = center
        ext[:, 7:8, :] = rows(64 + 2 * p, 1)
        ext[:, 24:25, :] = rows(65 + 2 * p, 1)
        grad_x = along_z(rows(16 * p, 16))
        grad_y = along_z(ext[:, 9:25, :] - ext[:, 7:23, :])
        pore = along_z(center)
        grad_z = after(pore) - before(pore)
        square = grad_x * grad_x + grad_y * grad_y + grad_z * grad_z + 0.01
        surface = square * lax.rsqrt(square)
        x_ref[:, 16 * p : 16 * p + 16, :] = surface
        x_ref[:, 32 + 16 * p : 48 + 16 * p, :] = pore
    parts = real_transform([x_ref[d] for d in range(16)])
    sign = jnp.where(lax.broadcasted_iota(jnp.int32, (128, 128), 1) < 64, 1.0, -1.0)

    def arranged(k):
        re, im = parts[k]
        if im is None:
            im = jnp.zeros_like(re)
        top = jnp.concatenate([re, im], axis=1)
        bottom = jnp.concatenate([im, -re], axis=1)
        high, low = split(jnp.concatenate([top, bottom], axis=0))
        return jnp.concatenate([high, high, low], axis=1)

    for k in range(9):
        wave = dot_t(w_ref[k], arranged(k))
        out_ref[k] = wave
        if 0 < k < 8:
            wave = wave * sign
            for block in range(16):
                out_ref[16 - k, 8 * block : 8 * block + 8, :] = wave[120 - 8 * block : 128 - 8 * block]


def modes_kernel(in_ref, y_ref, tr_ref, ti_ref, last_ref, out_ref):
    tr, ti = tr_ref[...], ti_ref[...]
    turned = jnp.concatenate([in_ref[pl.ds(q, 256, stride=8), :].T for q in range(8)], axis=0)
    halves_of_modes = []
    for odd in range(2):
        high, low = split(turned[:, :128] - turned[:, 128:] if odd else turned[:, :128] + turned[:, 128:])
        part = dot(jnp.concatenate([high, high, low], axis=1), y_ref[384 * odd : 384 * odd + 384, :])
        halves_of_modes.append(part)
    for q in range(8):
        parts = [part[128 * q : 128 * q + 128] for part in halves_of_modes]
        cos = jnp.concatenate([part[:, :128] for part in parts], axis=1)
        sin = jnp.concatenate([part[:, 128:] for part in parts], axis=1)
        high, low = split(jnp.concatenate([cos * tr + sin * ti, sin * tr - cos * ti], axis=0))
        modes = dot(last_ref[...], jnp.concatenate([high, high, low], axis=0))
        sr, si, pr, pi = modes[:32], modes[32:64], modes[64:96], modes[96:]
        square = sr * sr + si * si
        some = square > 1e-30
        scale = lax.rsqrt(jnp.maximum(square, 1e-30))
        results = (
            square * scale,
            jnp.where(some, (sr * pr + si * pi) * scale, jnp.sqrt(pr * pr + pi * pi)),
            jnp.where(some, (si * pr - sr * pi) * scale, 0.0),
        )
        for o, result in enumerate(results):
            for p in range(2):
                for half in range(2):
                    block = result[16 * p : 16 * p + 16, 128 * half : 128 * half + 128]
                    out_ref[pl.ds(place(o, p, half, q), 16, stride=96), :] = block


def place(o, p, half, q):
    return 32 * o + 16 * p + 8 * half + q


def spectra_kernel(in_ref, out_ref, held, sems):
    factor = 64.0 / (4096 * 2048)
    row = lax.broadcasted_iota(jnp.int32, (128, 128), 0)
    col = lax.broadcasted_iota(jnp.int32, (128, 128), 1)
    device = lax.axis_index("gy") + lax.axis_index("gz")
    drop = row + col + device == 0
    eighth = lax.broadcasted_iota(jnp.int32, (8, 128), 0) == 0

    def received(o, p, odd):
        blocks = [in_ref[pl.ds(place(o, p, odd, q), 16, stride=96), :] for q in range(8)]
        upper = [jnp.where(eighth, blocks[q][8:], blocks[7 - q][8:]) for q in range(8)]
        return jnp.concatenate([half for q in range(8) for half in (blocks[q][:8], upper[q])], axis=0)

    copies = []
    for p in range(2):
        for odd in range(2):
            size, re, im = [received(o, p, odd).T for o in range(3)]
            scaled = size * factor
            results = (size * scaled, (re * re + im * im) * factor, scaled * re, scaled * im)
            for o, result in enumerate(results):
                result = result if odd else jnp.where(drop, 0.0, result)
                held[pl.ds(256 * (4 * p + o) + odd, 128, stride=2), :] = result
                if odd:
                    source = held.at[pl.ds(256 * (4 * p + o), 256), :]
                    copies.append(pltpu.make_async_copy(source, out_ref.at[o, p], sems.at[4 * p + o]))
                    copies[-1].start()
    for copy in copies:
        copy.wait()


def shape(*sizes):
    return jax.ShapeDtypeStruct(sizes, jnp.float32)


def shards(labels, porosity):
    count = lax.axis_size("gy")
    following = lax.ppermute(labels[:, :4, :], "gy", [((i + 1) % count, i) for i in range(count)])
    planes, ends, table = pl.pallas_call(
        planes_kernel,
        out_shape=(shape(16 * CHUNK, 128), shape(4, 24, 128), shape(8, 128)),
        in_specs=[HBM, HBM],
        out_specs=(VMEM, VMEM, VMEM),
        scratch_shapes=[
            pltpu.VMEM((6, 256, 128), jnp.int32),
            pltpu.SMEM((6,), jnp.float32),
            pltpu.VMEM((4, 256, 128), jnp.float32),
            pltpu.SemaphoreType.DMA((BLOCKS + 1,)),
        ],
        compiler_params=PARAMS,
        cost_estimate=pl.CostEstimate(flops=10_000_000, bytes_accessed=4_000_000, transcendentals=0),
        name="planes",
    )(*[pltpu.with_memory_space_constraint(array, pltpu.HBM) for array in (porosity, labels)])
    rows = pl.pallas_call(
        rows_kernel,
        out_shape=shape(16 * CHUNK, 128),
        in_specs=[VMEM, VMEM, VMEM, VMEM],
        out_specs=VMEM,
        scratch_shapes=[pltpu.VMEM((4, 32, 128), jnp.float32)],
        compiler_params=PARAMS,
        name="rows",
    )(planes, ends, table, following)
    rows = lax.all_to_all(rows.reshape(4 * CHUNK, 4, 128), "gz", 0, 0, tiled=True).reshape(16 * CHUNK, 128)
    columns = pl.pallas_call(
        columns_kernel,
        out_shape=shape(16, 128, 128),
        in_specs=[VMEM, VMEM],
        out_specs=VMEM,
        scratch_shapes=[pltpu.VMEM((16, 32, 128), jnp.float32), pltpu.VMEM((16, 64, 128), jnp.float32)],
        compiler_params=PARAMS,
        name="columns",
    )(rows, jnp.asarray(z_matrices()))
    columns = lax.all_to_all(columns.reshape(256, 8, 128), ("gy", "gz"), 0, 0, tiled=True)
    cos, sin = twiddles()
    modes = pl.pallas_call(
        modes_kernel,
        out_shape=shape(16 * 96, 128),
        in_specs=[VMEM] * 5,
        out_specs=VMEM,
        compiler_params=PARAMS,
        name="modes",
    )(columns.reshape(2048, 128), jnp.asarray(y_matrix()), jnp.asarray(cos), jnp.asarray(sin), jnp.asarray(last_matrix()))
    modes = lax.all_to_all(modes.reshape(16, 96, 128), "gy", 0, 0, tiled=True)
    return pl.pallas_call(
        spectra_kernel,
        out_shape=shape(4, 2, 256, 128),
        in_specs=[VMEM],
        out_specs=HBM,
        scratch_shapes=[pltpu.VMEM((8 * 256, 128), jnp.float32), pltpu.SemaphoreType.DMA((8,))],
        compiler_params=PARAMS,
        name="spectra",
    )(modes.reshape(16 * 96, 128))


def solution(mesh):
    placed = (P(None, "gy", "gz"), P())
    return jax.shard_map(
        shards, mesh=mesh, in_specs=placed, out_specs=P(None, None, "gy", "gz"), check_vma=False
    )
```

```python
import functools
import math

import jax
import jax.numpy as jnp
import ml_dtypes
import numpy as np
from jax import lax
from jax.experimental import pallas as pl
from jax.experimental.pallas import tpu as pltpu
from jax.sharding import PartitionSpec as P

VMEM = pl.BlockSpec(memory_space=pltpu.VMEM)
HBM = pl.BlockSpec(memory_space=pltpu.HBM)
PARAMS = pltpu.CompilerParams(vmem_limit_bytes=48 * 1024 * 1024)


def halves(matrix):
    high = matrix.astype(ml_dtypes.bfloat16)
    low = (matrix - high.astype(np.float64)).astype(ml_dtypes.bfloat16)
    return high, low


def split(value):
    high = value.astype(jnp.bfloat16)
    low = (value - high.astype(jnp.float32)).astype(jnp.bfloat16)
    return high, low


def dot(a, b):
    return lax.dot_general(a, b, (((1,), (0,)), ((), ())), preferred_element_type=jnp.float32)


def dot_t(a, b):
    return lax.dot_general(a, b, (((1,), (1,)), ((), ())), preferred_element_type=jnp.float32)


def joined(matrix, axis):
    high, low = halves(matrix)
    return np.concatenate([high, low, high], axis=axis)


def z_matrices():
    q = np.arange(128)[:, None]
    j = np.arange(128)[None, :]
    angles = [2.0 * math.pi / 2048 * ((j * (16 * q + s)) % 2048) for s in range(9)]
    return np.stack([joined(np.concatenate([np.cos(t), np.sin(t)], axis=1), 1) for t in angles])


def y_matrix():
    i = np.arange(128)[:, None]
    blocks = []
    for odd in range(2):
        m = 2 * np.arange(128)[None, :] + odd
        theta = 2.0 * math.pi / 256 * ((i * m) % 256)
        blocks.append(joined(np.concatenate([np.cos(theta), np.sin(theta)], axis=1), 0))
    return np.concatenate(blocks, axis=0)


def twiddles():
    r = np.arange(128)[:, None] % 16
    m = np.concatenate([np.arange(0, 256, 2), np.arange(1, 256, 2)])[None, :]
    phi = 2.0 * math.pi / 4096 * (m * r)
    return np.cos(phi).astype(np.float32), (-np.sin(phi)).astype(np.float32)


def last_matrix():
    w = np.zeros((4, 2, 16, 2, 2, 2, 2, 16))
    g = np.arange(16)[:, None]
    r = np.arange(16)[None, :]
    psi = 2.0 * math.pi / 16 * ((g * r) % 16)
    cos, sin = np.cos(psi), np.sin(psi)
    for field in range(2):
        for plane in range(2):
            w[2 * field, plane, :, 0, 0, field, plane] = cos
            w[2 * field, plane, :, 1, 1, field, plane] = cos
            w[2 * field, plane, :, 0, 1, field, plane] = sin
            w[2 * field, plane, :, 1, 0, field, plane] = -sin
            w[2 * field + 1, plane, :, 0, 1, field, plane] = cos
            w[2 * field + 1, plane, :, 1, 0, field, plane] = -cos
            w[2 * field + 1, plane, :, 0, 0, field, plane] = -sin
            w[2 * field + 1, plane, :, 1, 1, field, plane] = -sin
    return joined(w.reshape(128, 256), 1)


def fill(values, ids):
    value = jnp.where(ids == 1, values[1], values[0])
    for k in range(2, 6):
        value = jnp.where(ids == k, values[k], value)
    return value


def along_x(f):
    s = [(f[k] + 6.0 * f[k + 1] + f[k + 2]) * 0.125 for k in range(4)]
    return [s[2] - s[0], s[3] - s[1], s[1], s[2]]


def along_y(ext, a, first, count):
    return (
        ext[a, first + 1 : first + 1 + count, :]
        + 6.0 * ext[a, first + 2 : first + 2 + count, :]
        + ext[a, first + 3 : first + 3 + count, :]
    ) * 0.125


CHUNK = 68
BLOCKS = 8
TALL = 256 // BLOCKS


def planes_kernel(por_ref, lab_ref, out_ref, end_ref, table_ref, held, few, ext, sems):
    copies = [pltpu.make_async_copy(por_ref, few, sems.at[BLOCKS])]
    for b in range(BLOCKS):
        rows = pl.ds(TALL * b, TALL)
        copies.append(pltpu.make_async_copy(lab_ref.at[:, rows, :], held.at[:, rows, :], sems.at[b]))
    for copy in copies:
        copy.start()
    copies[0].wait()
    values = [few[k] for k in range(6)]
    for k in range(6):
        table_ref[k : k + 1, :] = jnp.full((1, 128), values[k], jnp.float32)
    table_ref[6:8, :] = jnp.zeros((2, 128), jnp.float32)
    done = 0
    for b in range(BLOCKS):
        copies[1 + b].wait()
        rows = pl.ds(TALL * b, TALL)
        for a, value in enumerate(along_x([fill(values, held[x, rows, :]) for x in range(6)])):
            ext[a, rows, :] = value
        ready = (TALL * (b + 1) - 3) // 16
        for a in range(4):
            for d in range(done, ready):
                at = CHUNK * d + 16 * a
                out_ref[at : at + 16, :] = along_y(ext, a, 16 * d, 16)
        done = ready
    for p in range(2):
        a = 2 + p
        for d in range(15):
            at = CHUNK * d + 16 * a
            edge = CHUNK * d + 64 + 2 * p
            below = along_y(ext, a, -1, 1) if d == 0 else out_ref[at - CHUNK + 15 : at - CHUNK + 16, :]
            above = along_y(ext, a, 240, 1) if d == 14 else out_ref[at + CHUNK : at + CHUNK + 1, :]
            out_ref[edge : edge + 1, :] = below
            out_ref[edge + 1 : edge + 2, :] = above
    out_ref[15 * CHUNK :, :] = jnp.zeros((CHUNK, 128), jnp.float32)
    end_ref[...] = ext[:, 232:256, :]


def rows_kernel(in_ref, end_ref, table_ref, next_ref, out_ref, ext):
    last = 15 * CHUNK
    out_ref[:last, :] = in_ref[:last, :]
    ext[:, 0:24, :] = end_ref[...]
    values = [table_ref[k : k + 1, :] for k in range(6)]
    for a, value in enumerate(along_x([fill(values, next_ref[x]) for x in range(6)])):
        ext[a, 24:28, :] = value
        out_ref[last + 16 * a : last + 16 * a + 16, :] = along_y(ext, a, 8, 16)
    for p in range(2):
        a = 2 + p
        edge = last + 64 + 2 * p
        out_ref[edge : edge + 1, :] = along_y(ext, a, 7, 1)
        out_ref[edge + 1 : edge + 2, :] = along_y(ext, a, 24, 1)


def real_transform(x):
    n = len(x)
    if n == 2:
        return [(x[0] + x[1], None), (x[0] - x[1], None)]
    even = real_transform(x[0::2])
    odd = real_transform(x[1::2])
    out = [None] * (n // 2 + 1)
    for k in range(n // 4 + 1):
        (er, ei), (dr, di) = even[k], odd[k]
        c, s = math.cos(2.0 * math.pi * k / n), math.sin(2.0 * math.pi * k / n)
        if k == 0:
            out[0] = (er + dr, None)
            out[n // 2] = (er - dr, None)
        elif 4 * k == n:
            out[k] = (er, -dr)
        else:
            tr = c * dr if di is None else c * dr + s * di
            ti = -s * dr if di is None else c * di - s * dr
            out[k] = (er + tr, ti if ei is None else ei + ti)
            out[n // 2 - k] = (er - tr, ti if ei is None else ti - ei)
    return out


def columns_kernel(in_ref, w_ref, out_ref, ext, x_ref):
    lane = lax.broadcasted_iota(jnp.int32, (16, 16, 128), 2)

    def before(x):
        rolled = pltpu.roll(x, 1, 2)
        return jnp.where(lane == 0, jnp.concatenate([rolled[15:], rolled[:15]], axis=0), rolled)

    def after(x):
        rolled = pltpu.roll(x, 127, 2)
        return jnp.where(lane == 127, jnp.concatenate([rolled[1:], rolled[:1]], axis=0), rolled)

    def along_z(x):
        return (before(x) + 6.0 * x + after(x)) * 0.125

    def rows(first, count):
        return jnp.stack([in_ref[CHUNK * d + first : CHUNK * d + first + count, :] for d in range(16)])

    for p in range(2):
        center = rows(32 + 16 * p, 16)
        ext[:, 8:24, :] = center
        ext[:, 7:8, :] = rows(64 + 2 * p, 1)
        ext[:, 24:25, :] = rows(65 + 2 * p, 1)
        grad_x = along_z(rows(16 * p, 16))
        grad_y = along_z(ext[:, 9:25, :] - ext[:, 7:23, :])
        pore = along_z(center)
        grad_z = after(pore) - before(pore)
        square = grad_x * grad_x + grad_y * grad_y + grad_z * grad_z + 0.01
        surface = square * lax.rsqrt(square)
        x_ref[:, 16 * p : 16 * p + 16, :] = surface
        x_ref[:, 32 + 16 * p : 48 + 16 * p, :] = pore
    parts = real_transform([x_ref[d] for d in range(16)])
    sign = jnp.where(lax.broadcasted_iota(jnp.int32, (128, 128), 1) < 64, 1.0, -1.0)

    def arranged(k):
        re, im = parts[k]
        if im is None:
            im = jnp.zeros_like(re)
        top = jnp.concatenate([re, im], axis=1)
        bottom = jnp.concatenate([im, -re], axis=1)
        high, low = split(jnp.concatenate([top, bottom], axis=0))
        return jnp.concatenate([high, high, low], axis=1)

    for k in range(9):
        wave = dot_t(w_ref[k], arranged(k))
        out_ref[k] = wave
        if 0 < k < 8:
            wave = wave * sign
            for block in range(16):
                out_ref[16 - k, 8 * block : 8 * block + 8, :] = wave[120 - 8 * block : 128 - 8 * block]


def modes_kernel(in_ref, y_ref, tr_ref, ti_ref, last_ref, out_ref):
    tr, ti = tr_ref[...], ti_ref[...]
    turned = jnp.concatenate([in_ref[pl.ds(q, 256, stride=8), :].T for q in range(8)], axis=0)
    halves_of_modes = []
    for odd in range(2):
        high, low = split(turned[:, :128] - turned[:, 128:] if odd else turned[:, :128] + turned[:, 128:])
        part = dot(jnp.concatenate([high, high, low], axis=1), y_ref[384 * odd : 384 * odd + 384, :])
        halves_of_modes.append(part)
    for q in range(8):
        parts = [part[128 * q : 128 * q + 128] for part in halves_of_modes]
        cos = jnp.concatenate([part[:, :128] for part in parts], axis=1)
        sin = jnp.concatenate([part[:, 128:] for part in parts], axis=1)
        high, low = split(jnp.concatenate([cos * tr + sin * ti, sin * tr - cos * ti], axis=0))
        modes = dot(last_ref[...], jnp.concatenate([high, high, low], axis=0))
        sr, si, pr, pi = modes[:32], modes[32:64], modes[64:96], modes[96:]
        square = sr * sr + si * si
        some = square > 1e-30
        scale = lax.rsqrt(jnp.maximum(square, 1e-30))
        results = (
            square * scale,
            jnp.where(some, (sr * pr + si * pi) * scale, jnp.sqrt(pr * pr + pi * pi)),
            jnp.where(some, (si * pr - sr * pi) * scale, 0.0),
        )
        for o, result in enumerate(results):
            for p in range(2):
                for half in range(2):
                    block = result[16 * p : 16 * p + 16, 128 * half : 128 * half + 128]
                    out_ref[pl.ds(place(o, p, half, q), 16, stride=96), :] = block


def place(o, p, half, q):
    return 32 * o + 16 * p + 8 * half + q


def spectra_kernel(in_ref, out_ref, held, sems):
    factor = 64.0 / (4096 * 2048)
    row = lax.broadcasted_iota(jnp.int32, (128, 128), 0)
    col = lax.broadcasted_iota(jnp.int32, (128, 128), 1)
    device = lax.axis_index("gy") + lax.axis_index("gz")
    drop = row + col + device == 0
    eighth = lax.broadcasted_iota(jnp.int32, (8, 128), 0) == 0

    def received(o, p, odd):
        blocks = [in_ref[pl.ds(place(o, p, odd, q), 16, stride=96), :] for q in range(8)]
        upper = [jnp.where(eighth, blocks[q][8:], blocks[7 - q][8:]) for q in range(8)]
        return jnp.concatenate([half for q in range(8) for half in (blocks[q][:8], upper[q])], axis=0)

    copies = []
    for p in range(2):
        for odd in range(2):
            size, re, im = [received(o, p, odd).T for o in range(3)]
            scaled = size * factor
            results = (size * scaled, (re * re + im * im) * factor, scaled * re, scaled * im)
            for o, result in enumerate(results):
                result = result if odd else jnp.where(drop, 0.0, result)
                held[pl.ds(256 * (4 * p + o) + odd, 128, stride=2), :] = result
                if odd:
                    source = held.at[pl.ds(256 * (4 * p + o), 256), :]
                    copies.append(pltpu.make_async_copy(source, out_ref.at[o, p], sems.at[4 * p + o]))
                    copies[-1].start()
    for copy in copies:
        copy.wait()


def shape(*sizes):
    return jax.ShapeDtypeStruct(sizes, jnp.float32)


def shards(labels, porosity):
    count = lax.axis_size("gy")
    following = lax.ppermute(labels[:, :4, :], "gy", [((i + 1) % count, i) for i in range(count)])
    planes, ends, table = pl.pallas_call(
        planes_kernel,
        out_shape=(shape(16 * CHUNK, 128), shape(4, 24, 128), shape(8, 128)),
        in_specs=[HBM, HBM],
        out_specs=(VMEM, VMEM, VMEM),
        scratch_shapes=[
            pltpu.VMEM((6, 256, 128), jnp.int32),
            pltpu.SMEM((6,), jnp.float32),
            pltpu.VMEM((4, 256, 128), jnp.float32),
            pltpu.SemaphoreType.DMA((BLOCKS + 1,)),
        ],
        compiler_params=PARAMS,
        cost_estimate=pl.CostEstimate(flops=10_000_000, bytes_accessed=4_000_000, transcendentals=0),
        name="planes",
    )(*[pltpu.with_memory_space_constraint(array, pltpu.HBM) for array in (porosity, labels)])
    rows = pl.pallas_call(
        rows_kernel,
        out_shape=shape(16 * CHUNK, 128),
        in_specs=[VMEM, VMEM, VMEM, VMEM],
        out_specs=VMEM,
        scratch_shapes=[pltpu.VMEM((4, 32, 128), jnp.float32)],
        compiler_params=PARAMS,
        name="rows",
    )(planes, ends, table, following)
    rows = lax.all_to_all(rows.reshape(4 * CHUNK, 4, 128), "gz", 0, 0, tiled=True).reshape(16 * CHUNK, 128)
    columns = pl.pallas_call(
        columns_kernel,
        out_shape=shape(16, 128, 128),
        in_specs=[VMEM, VMEM],
        out_specs=VMEM,
        scratch_shapes=[pltpu.VMEM((16, 32, 128), jnp.float32), pltpu.VMEM((16, 64, 128), jnp.float32)],
        compiler_params=PARAMS,
        name="columns",
    )(rows, jnp.asarray(z_matrices()))
    columns = lax.all_to_all(columns.reshape(256, 8, 128), ("gy", "gz"), 0, 0, tiled=True)
    cos, sin = twiddles()
    modes = pl.pallas_call(
        modes_kernel,
        out_shape=shape(16 * 96, 128),
        in_specs=[VMEM] * 5,
        out_specs=VMEM,
        compiler_params=PARAMS,
        name="modes",
    )(columns.reshape(2048, 128), jnp.asarray(y_matrix()), jnp.asarray(cos), jnp.asarray(sin), jnp.asarray(last_matrix()))
    modes = lax.all_to_all(modes.reshape(16, 96, 128), "gy", 0, 0, tiled=True)
    return pl.pallas_call(
        spectra_kernel,
        out_shape=shape(4, 2, 256, 128),
        in_specs=[VMEM],
        out_specs=HBM,
        scratch_shapes=[pltpu.VMEM((8 * 256, 128), jnp.float32), pltpu.SemaphoreType.DMA((8,))],
        compiler_params=PARAMS,
        name="spectra",
    )(modes.reshape(16 * 96, 128))


def solution(mesh):
    placed = (P(None, "gy", "gz"), P())
    return jax.shard_map(
        shards, mesh=mesh, in_specs=placed, out_specs=P(None, None, "gy", "gz"), check_vma=False
    )
```
